32 devices in a mesh: wide: 16 (over z, x, core), head: 2 (over y).
Axes of the slice: x: 2, y: 2, z: 4, core: 2. Of those that a mesh axis runs over, the one named last changes fastest.
Arguments:
- branch_query: bfloat16 [64, 8192], P('wide', 'head'), may hold values from -6 to 6
- key_new: bfloat16 [64, 1024], P('wide', 'head'), may hold values from -6 to 6
- value_new: bfloat16 [64, 1024], P('wide', 'head'), may hold values from -6 to 6
- pool_pages: bfloat16 [2, 1024, 16, 1024], P(None, 'wide', None, 'head'), may hold values from -6 to 6
- page_table: int32 [64, 16], P('wide'), may hold values from 0 to 63, as said below
- tail_length: int32 [64], P('wide'), may hold values from 1 to 256
- parent_row: int32 [64], P('wide'), may hold values from 0 to 63, as said below
- residual: bfloat16 [64, 8192], P(('wide', 'head')), may hold values from -6 to 6
- norm_gain: float32 [8192], replicated, may hold values from 0.5 to 1.5
- gate_blocks: bfloat16 [128, 32, 128, 128], P('wide'), may hold values from -0.09375 to 0.09375
- up_blocks: bfloat16 [128, 32, 128, 128], P('wide'), may hold values from -0.09375 to 0.09375
- gate_up_keep: int32 [128, 32], P('wide'), may hold values from 0 to 63, as said below
- gate_scale: float32 [128, 32], P('wide'), may hold values from 0.5 to 2
- up_scale: float32 [128, 32], P('wide'), may hold values from 0.5 to 2
- down_blocks: bfloat16 [128, 32, 128, 128], P('wide'), may hold values from -0.0625 to 0.0625
- down_keep: int32 [128, 32], P('wide'), may hold values from 0 to 63, as said below
- down_scale: float32 [128, 32], P('wide'), may hold values from 0.5 to 2
Outputs:
- layer_out: bfloat16 [64, 8192], P(('wide', 'head'))
The draws below stay inside these ranges and needn't reach their ends.
Inputs may be any that keep to these rules, and one draw needn't show every extreme that they name: parent_row never falls with the branch index, and parent_row[b] <= b and parent_row[b] > b - 4. `page_table`: the entries of the 4 rows held by one index of wide name each of that index's 64 pages once. `gate_up_keep`: each row names 32 different blocks. `down_keep`: each row names 32 different blocks.
All inputs are finite; a program needn't handle non-finite values.
Results may differ from the reference program's by a relative error of at most 0.017.
Values may be sent and summed in bfloat16 or wider, within the bound.
No kernel may reach another device: no remote copies, remote signals or barrier semaphores. Data moves between devices by JAX's collectives and lax.ppermute only.
A program may use at most 64 MiB of HBM per device.

```python
import math
import jax
import jax.numpy as jnp
from jax import lax

D = 8192
QH = 64
KVH = 8
HD = 128
FF = 16384
BLK = 128
KEEP = 32
PAGE = 16
TPAGES = 16
ROW_DEV = 4
ROWS = 64
TAIL = 256
POOL_DEV = 64
POOL = 1024
NBD = 64
NCB = 128


def base_normal(key, shape):
    return jnp.clip(jax.random.normal(key, shape, jnp.float32), -6.0, 6.0)


def draw_branch_query(key, part):
    sub_key = jax.random.fold_in(key, 31)
    base = base_normal(sub_key, (ROWS, QH, HD))
    return base.reshape(ROWS, QH * HD).astype(jnp.bfloat16)


def draw_key_new(key, part):
    sub_key = jax.random.fold_in(key, 32)
    base = base_normal(sub_key, (ROWS, KVH, HD))
    return base.reshape(ROWS, KVH * HD).astype(jnp.bfloat16)


def draw_pool_pages(key, part):
    sub_key = jax.random.fold_in(key, 33)
    base = base_normal(sub_key, (2, POOL, PAGE, KVH, HD))
    return base.reshape(2, POOL, PAGE, KVH * HD).astype(jnp.bfloat16)


def draw_residual(key, part):
    sub_key = jax.random.fold_in(key, 34)
    base = base_normal(sub_key, (ROWS, D))
    row_scale = jnp.exp(jax.random.uniform(jax.random.fold_in(key, 35), (ROWS, 1), jnp.float32, math.log(0.03), math.log(0.3)))
    col_scale = jnp.exp(jax.random.uniform(jax.random.fold_in(key, 36), (1, D), jnp.float32, math.log(0.3), math.log(3.0)))
    return (base * row_scale * col_scale).astype(jnp.bfloat16)


def draw_page_table(key, part):
    keys_all = jax.random.split(jax.random.fold_in(key, 13), ROWS // ROW_DEV)
    perms = jax.vmap(lambda one_key: jax.random.permutation(one_key, POOL_DEV))(keys_all)
    return perms.reshape(ROWS, TPAGES).astype(jnp.int32)


def draw_tail_length(key, part):
    lengths = jax.random.randint(jax.random.fold_in(key, 14), (ROWS,), 1, TAIL + 1, jnp.int32)
    lengths = lengths.at[::ROW_DEV].set(TAIL)
    lengths = lengths.at[1].set(1)
    return lengths


def draw_parent_row(key, part):
    delta = jax.random.randint(jax.random.fold_in(key, 15), (ROWS,), 0, ROW_DEV, jnp.int32)
    row_ids = jnp.arange(ROWS, dtype=jnp.int32)
    first_rows = (row_ids % ROW_DEV == 0) & (row_ids > 0)
    delta = jnp.where(first_rows, jnp.maximum(delta, 1), delta)
    candidate = jnp.maximum(row_ids - delta, 0)
    candidate = candidate.at[ROWS - 1].set(ROWS - 1)
    return lax.cummax(candidate, axis=0).astype(jnp.int32)


def keep_lists(key):
    keys_all = jax.random.split(key, NCB)
    perms = jax.vmap(lambda one_key: jax.random.permutation(one_key, NBD))(keys_all)
    return perms[:, :KEEP].astype(jnp.int32)


def draw_gate_up_keep(key, part):
    return keep_lists(jax.random.fold_in(key, 11))


def draw_down_keep(key, part):
    return keep_lists(jax.random.fold_in(key, 12))


def block_scale(stream_key, extent, cuts, smallest, high):
    factor_of, own = 1.0, jax.random.fold_in(stream_key, 6)
    for dim, shards_of in cuts:
        heights = jnp.exp(jax.random.uniform(jax.random.fold_in(own, dim), (shards_of,), jnp.float32, smallest / len(cuts), high / len(cuts)))
        factor_of = factor_of * jnp.repeat(heights, extent[dim] // shards_of).reshape([-1 if axis == dim else 1 for axis in range(len(extent))])
    return factor_of


def centred(key, shape, scale, reach, shards=(), kind=jnp.bfloat16):
    values = scale * jax.random.normal(key, shape, jnp.float32)
    if shards:
        values = values * block_scale(key, shape, shards, -0.22, 0.18)
    return jnp.clip(values, -reach, reach).astype(kind)


def setup_inputs(seed: int = 0) -> dict:
    seeds = jax.random.split(jax.random.key(seed), 18)
    return {
        "branch_query": draw_branch_query(jax.random.fold_in(seeds[17], 71), 0),
        "key_new": draw_key_new(jax.random.fold_in(seeds[17], 71), 0),
        "value_new": centred(seeds[2], (ROWS, KVH * HD), 1.0, 6.0, ((0, 16), (1, 2))),
        "pool_pages": draw_pool_pages(jax.random.fold_in(seeds[17], 71), 0),
        "page_table": draw_page_table(jax.random.fold_in(seeds[17], 71), 0),
        "tail_length": draw_tail_length(jax.random.fold_in(seeds[17], 71), 0),
        "parent_row": draw_parent_row(jax.random.fold_in(seeds[17], 71), 0),
        "residual": draw_residual(jax.random.fold_in(seeds[17], 71), 0),
        "norm_gain": jnp.clip(1.0 + 0.1 * jax.random.normal(seeds[8], (D,), jnp.float32), 0.5, 1.5),
        "gate_blocks": centred(seeds[9], (NCB, KEEP, BLK, BLK), (KEEP * BLK) ** -0.5, 0.09375, ((0, 16),)),
        "up_blocks": centred(seeds[10], (NCB, KEEP, BLK, BLK), (KEEP * BLK) ** -0.5, 0.09375, ((0, 16),)),
        "gate_up_keep": draw_gate_up_keep(jax.random.fold_in(seeds[17], 71), 0),
        "gate_scale": jnp.clip(jnp.exp(math.log(2.0) - 1.3862944 * jax.random.uniform(seeds[12], (NCB, KEEP), jnp.float32) ** block_scale(seeds[12], (NCB, KEEP), ((0, 16),), -0.2, 0.2)), 0.5, 2.0),
        "up_scale": jnp.clip(jnp.exp(math.log(2.0) - 1.3862944 * jax.random.uniform(seeds[13], (NCB, KEEP), jnp.float32) ** block_scale(seeds[13], (NCB, KEEP), ((0, 16),), -0.2, 0.2)), 0.5, 2.0),
        "down_blocks": centred(seeds[14], (NCB, KEEP, BLK, BLK), (FF // 2) ** -0.5, 0.0625, ((0, 16),)),
        "down_keep": draw_down_keep(jax.random.fold_in(seeds[17], 71), 0),
        "down_scale": jnp.clip(jnp.exp(math.log(2.0) - 1.3862944 * jax.random.uniform(seeds[16], (NCB, KEEP), jnp.float32) ** block_scale(seeds[16], (NCB, KEEP), ((0, 16),), -0.2, 0.2)), 0.5, 2.0),
    }


def reference(branch_query, key_new, value_new, pool_pages, page_table, tail_length, parent_row, residual, norm_gain, gate_blocks, up_blocks, gate_up_keep, gate_scale, up_scale, down_blocks, down_keep, down_scale):
    per_group = QH // KVH
    factor = 1.0 / math.sqrt(HD)
    pool_keys = pool_pages[0]
    pool_values = pool_pages[1]
    highest_prec = lax.Precision.HIGHEST

    def one_branch(branch):
        parent_index = parent_row[branch]
        owner = parent_index // ROW_DEV
        pages = (owner * POOL_DEV + page_table[parent_index]).astype(jnp.int32)
        tail_keys = pool_keys[pages].reshape(TAIL, KVH, HD)
        tail_values = pool_values[pages].reshape(TAIL, KVH, HD)
        keys_all = jnp.concatenate([tail_keys, key_new[branch].reshape(1, KVH, HD)], axis=0).astype(jnp.float32)
        values_all = jnp.concatenate([tail_values, value_new[branch].reshape(1, KVH, HD)], axis=0).astype(jnp.float32)
        queries = branch_query[branch].reshape(KVH, per_group, HD).astype(jnp.float32)
        scores = jnp.einsum('gjd,tgd->gjt', queries, keys_all, precision=highest_prec) * factor
        length = tail_length[parent_index]
        live_mask = jnp.concatenate([jnp.arange(TAIL, dtype=jnp.int32) < length, jnp.ones((1,), dtype=bool)])
        top_score = lax.optimization_barrier(jnp.max(jnp.where(live_mask, scores, -1e+30), axis=-1))
        expo = jnp.where(live_mask, jnp.exp(scores - top_score[..., None]), 0.0)
        weights_all = (expo / lax.optimization_barrier(jnp.sum(expo, axis=-1))[..., None]).astype(jnp.bfloat16)
        mixture = jnp.einsum('gjt,tgd->gjd', weights_all.astype(jnp.float32), values_all, precision=highest_prec)
        return mixture.reshape(QH * HD).astype(jnp.bfloat16)
    attention = lax.map(one_branch, jnp.arange(ROWS, dtype=jnp.int32))
    middle = residual.astype(jnp.float32) + attention.astype(jnp.float32)
    normed = (middle * lax.rsqrt(lax.optimization_barrier(jnp.mean(middle * middle, axis=-1, keepdims=True)) + 1e-05) * norm_gain).astype(jnp.bfloat16)
    blocks = normed.reshape(ROWS, NBD, BLK)

    def column_step(accum, pieces):
        gate_w, up_w, keep_rows, gate_s, up_s, down_w, keep_cols, down_s = pieces
        picked = blocks[:, keep_rows].astype(jnp.float32)
        gate_sum = lax.optimization_barrier(jnp.sum(jnp.einsum('rkd,kdf->rkf', picked, gate_w.astype(jnp.float32), precision=highest_prec) * gate_s[None, :, None], axis=1))
        up_sum = lax.optimization_barrier(jnp.sum(jnp.einsum('rkd,kdf->rkf', picked, up_w.astype(jnp.float32), precision=highest_prec) * up_s[None, :, None], axis=1))
        hidden = (jax.nn.silu(gate_sum) * up_sum).astype(jnp.bfloat16)
        contrib = jnp.einsum('rf,kfe->rke', hidden.astype(jnp.float32), down_w.astype(jnp.float32), precision=highest_prec) * down_s[None, :, None]
        return (accum.at[:, keep_cols].add(contrib), None)
    start_acc = jnp.zeros((ROWS, NBD, BLK), jnp.float32)
    ffn_acc, _ = lax.scan(column_step, start_acc, (gate_blocks, up_blocks, gate_up_keep, gate_scale, up_scale, down_blocks, down_keep, down_scale))
    ffn_sum = ffn_acc.reshape(ROWS, D)
    return (middle + ffn_sum).astype(jnp.bfloat16)
```

```python
import functools
import math

import jax
import jax.numpy as jnp
from jax import lax
from jax.experimental import pallas as pl
from jax.experimental.pallas import tpu as pltpu
from jax.sharding import PartitionSpec as P

HD = 128
BLK = 128
DEAD = -1e30
MIB = 1024 * 1024

VMEM = pl.BlockSpec(memory_space=pltpu.VMEM)
SMEM = pl.BlockSpec(memory_space=pltpu.SMEM)
ANY = pl.BlockSpec(memory_space=pl.ANY)


def attend_kernel(
    groups, per_group, page_ref, length_ref, own_ref, next_ref, pool_ref,
    stay_ref, cross_ref, ahead_ref, ahead_cross_ref, mixed,
):
    rows = own_ref.shape[0]
    width = groups * per_group * HD
    kv_width = groups * HD
    pages, page = pool_ref.shape[1], pool_ref.shape[2]
    spots = pages * page
    head = lax.axis_index("head")

    spot = lax.broadcasted_iota(jnp.int32, (1, spots), 1)
    page_of, offset = spot // page, spot % page
    biases = []
    for r in range(rows):
        place = jnp.full((1, spots), 1 << 20, jnp.int32)
        for i in range(page_ref.shape[1]):
            place = jnp.where(page_of == page_ref[r, i], i * page, place)
        biases.append(jnp.where(place + offset < length_ref[r], 0.0, DEAD))

    both = jnp.concatenate(
        [own_ref[...].astype(jnp.float32), next_ref[...].astype(jnp.float32)], axis=0
    )
    shift = lax.broadcasted_iota(jnp.int32, (2 * rows, 1), 0) // rows * rows
    parent = both[:, width + 2 * kv_width : width + 2 * kv_width + 1] + shift.astype(jnp.float32)
    bias = jnp.full((2 * rows, spots), DEAD, jnp.float32)
    for r in range(rows):
        bias = jnp.where(parent == r, biases[r], bias)
    here = (parent >= 0) & (parent < rows)

    factor = 1.0 / math.sqrt(HD)
    for g in range(groups):
        base = g * per_group * HD
        query = jnp.concatenate(
            [both[:, base + j * HD : base + (j + 1) * HD] for j in range(per_group)], axis=0
        )
        key_own = both[:, width + g * HD : width + (g + 1) * HD]
        value_own = both[:, width + kv_width + g * HD : width + kv_width + (g + 1) * HD]
        keys = pool_ref[0, :, :, g * HD : (g + 1) * HD].reshape(spots, HD)
        values = pool_ref[1, :, :, g * HD : (g + 1) * HD].reshape(spots, HD)
        scores = lax.dot_general(
            query.astype(jnp.bfloat16), keys, (((1,), (1,)), ((), ())),
            preferred_element_type=jnp.float32,
        )
        scores = scores.reshape(per_group, 2 * rows, spots) * factor + bias[None]
        query = query.reshape(per_group, 2 * rows, HD)
        own = jnp.sum(query * key_own[None], axis=-1, keepdims=True) * factor
        top = jnp.maximum(jnp.max(scores, axis=-1, keepdims=True), own)
        expo = jnp.exp(scores - top)
        own_expo = jnp.exp(own - top)
        total = jnp.sum(expo, axis=-1, keepdims=True) + own_expo
        weights = (expo / total).astype(jnp.bfloat16)
        own_weight = (own_expo / total).astype(jnp.bfloat16).astype(jnp.float32)
        mixture = jnp.dot(
            weights.reshape(per_group * 2 * rows, spots), values,
            preferred_element_type=jnp.float32,
        )
        mixture = mixture.reshape(per_group, 2 * rows, HD) + own_weight * value_own[None]
        for j in range(per_group):
            mixed[:, base + j * HD : base + (j + 1) * HD] = jnp.where(here, mixture[j], 0.0)

    part = stay_ref.shape[0]
    for start, mine_ref, other_ref in ((0, stay_ref, cross_ref), (rows, ahead_ref, ahead_cross_ref)):
        low = mixed[start : start + part, :]
        high = mixed[start + part : start + 2 * part, :]
        mine_ref[...] = jnp.where(head == 0, low, high).astype(jnp.bfloat16)
        other_ref[...] = jnp.where(head == 0, high, low).astype(jnp.bfloat16)


def norm_kernel(
    stay_ref, cross_ref, behind_ref, behind_cross_ref, residual_ref, gain_ref,
    middle_ref, normed_ref,
):
    head = lax.axis_index("head")
    half = stay_ref.shape[1]
    f32 = jnp.float32
    same = stay_ref[...].astype(f32) + behind_ref[...].astype(f32)
    other = cross_ref[...].astype(f32) + behind_cross_ref[...].astype(f32)
    first = jnp.where(head == 0, same, other)
    second = jnp.where(head == 0, other, same)
    low = residual_ref[:, :half].astype(f32) + first
    high = residual_ref[:, half:].astype(f32) + second
    middle_ref[:, :half] = low
    middle_ref[:, half:] = high
    square = jnp.sum(low * low, axis=-1, keepdims=True)
    square = square + jnp.sum(high * high, axis=-1, keepdims=True)
    scale = lax.rsqrt(square / (2 * half) + 1e-05)
    normed_ref[:, :half] = (low * scale * gain_ref[:, :half]).astype(jnp.bfloat16)
    normed_ref[:, half:] = (high * scale * gain_ref[:, half:]).astype(jnp.bfloat16)


def feed_kernel(
    keep_ref, gate_scale_ref, up_scale_ref, down_keep_ref, down_scale_ref,
    near_ref, far_ref, gate_hbm, up_hbm, down_hbm,
    stay_ref, send_ref,
    gate, up, down, total, sems,
):
    columns, keep = keep_ref.shape
    half = near_ref.shape[0]
    pairs = ((gate_hbm, gate), (up_hbm, up), (down_hbm, down))

    def fetch(which, c):
        source, target = pairs[which]
        return pltpu.make_async_copy(source.at[c], target.at[c], sems.at[which, c])

    def begin(c, carry):
        for which in range(3):
            fetch(which, c).start()
        return carry

    lax.fori_loop(0, columns, begin, 0)
    total[...] = jnp.zeros_like(total)

    def column(c, carry):
        fetch(0, c).wait()
        fetch(1, c).wait()
        gate_sum = jnp.zeros((2 * half, BLK), jnp.float32)
        up_sum = jnp.zeros((2 * half, BLK), jnp.float32)
        for k in range(keep):
            where = pl.ds(pl.multiple_of(keep_ref[c, k] * BLK, BLK), BLK)
            picked = jnp.concatenate([near_ref[:, where], far_ref[:, where]], axis=0)
            gate_sum += gate_scale_ref[c, k] * jnp.dot(
                picked, gate[c, k], preferred_element_type=jnp.float32
            )
            up_sum += up_scale_ref[c, k] * jnp.dot(
                picked, up[c, k], preferred_element_type=jnp.float32
            )
        hidden = (gate_sum / (1.0 + jnp.exp(-gate_sum)) * up_sum).astype(jnp.bfloat16)
        fetch(2, c).wait()
        for k in range(keep):
            where = pl.ds(pl.multiple_of(down_keep_ref[c, k] * BLK, BLK), BLK)
            total[:, where] += down_scale_ref[c, k] * jnp.dot(
                hidden, down[c, k], preferred_element_type=jnp.float32
            )
        return carry

    lax.fori_loop(0, columns, column, 0)
    stay_ref[...] = total[:half, :]
    send_ref[...] = total[half:, :].astype(jnp.bfloat16)


def swapped(block, bit):
    return lax.ppermute(block, "wide", [(i, i ^ bit) for i in range(lax.axis_size("wide"))])


def per_device(
    branch_query, key_new, value_new, pool_pages, page_table, tail_length, parent_row, residual,
    norm_gain, gate_blocks, up_blocks, gate_up_keep, gate_scale, up_scale, down_blocks, down_keep,
    down_scale,
):
    bf16, f32 = jnp.bfloat16, jnp.float32
    wide, heads = lax.axis_size("wide"), lax.axis_size("head")
    rows, width = branch_query.shape
    groups = key_new.shape[1] // HD
    per_group = width // (groups * HD)
    part = residual.shape[0]
    model = residual.shape[1]

    relative = (parent_row - lax.axis_index("wide") * rows).astype(bf16)
    own = jnp.concatenate(
        [branch_query, key_new, value_new, jnp.broadcast_to(relative[:, None], (rows, HD))], axis=1
    )
    following = lax.ppermute(own, "wide", [(i, i - 1) for i in range(1, wide)])
    piece = jax.ShapeDtypeStruct((part, width), bf16)
    stay, cross, ahead, ahead_cross = pl.pallas_call(
        functools.partial(attend_kernel, groups, per_group),
        out_shape=(piece,) * 4,
        in_specs=[SMEM, SMEM, VMEM, VMEM, VMEM],
        out_specs=(VMEM,) * 4,
        scratch_shapes=[pltpu.VMEM((2 * rows, width), f32)],
        compiler_params=pltpu.CompilerParams(vmem_limit_bytes=24 * MIB),
        name="attend",
    )(page_table, tail_length, own, following, pool_pages)

    cross = lax.ppermute(cross, "head", [(h, 1 - h) for h in range(heads)])
    behind = lax.ppermute(ahead, "wide", [(i, i + 1) for i in range(wide - 1)])
    behind_cross = lax.ppermute(
        ahead_cross,
        ("wide", "head"),
        [(i * heads + h, (i + 1) * heads + 1 - h) for i in range(wide - 1) for h in range(heads)],
    )
    middle, normed = pl.pallas_call(
        norm_kernel,
        out_shape=(
            jax.ShapeDtypeStruct((part, model), f32),
            jax.ShapeDtypeStruct((part, model), bf16),
        ),
        in_specs=[VMEM] * 6,
        out_specs=(VMEM,) * 2,
        compiler_params=pltpu.CompilerParams(vmem_limit_bytes=8 * MIB),
        name="norm",
    )(stay, cross, behind, behind_cross, residual, norm_gain.reshape(1, model))

    bits = [1 << b for b in range(wide.bit_length() - 1)]
    gathered = normed
    for bit in bits[:0:-1]:
        gathered = jnp.concatenate([gathered, swapped(gathered, bit)], axis=0)
    far = swapped(gathered, bits[0])

    half = gathered.shape[0]
    weights = [gate_blocks, up_blocks, down_blocks]
    size = 2 * half * model * 4 + half * model * 10 + sum(w.size * 2 for w in weights)
    kept, sent = pl.pallas_call(
        feed_kernel,
        out_shape=(
            jax.ShapeDtypeStruct((half, model), f32),
            jax.ShapeDtypeStruct((half, model), bf16),
        ),
        in_specs=[SMEM] * 5 + [VMEM] * 2 + [ANY] * 3,
        out_specs=(VMEM,) * 2,
        scratch_shapes=[pltpu.VMEM(w.shape, bf16) for w in weights]
        + [pltpu.VMEM((2 * half, model), f32), pltpu.SemaphoreType.DMA((3, gate_blocks.shape[0]))],
        compiler_params=pltpu.CompilerParams(vmem_limit_bytes=size + 8 * MIB),
        name="feed",
    )(
        gate_up_keep, gate_scale, up_scale, down_keep, down_scale,
        gathered, far, gate_blocks, up_blocks, down_blocks,
    )

    for bit in bits:
        summed = kept + swapped(sent, bit).astype(f32)
        if bit != bits[-1]:
            half = half // 2
            kept, sent = summed[:half], summed[half:].astype(bf16)
    return (middle + summed).astype(bf16)


def solution(mesh):
    placed = (
        P("wide", "head"),
        P("wide", "head"),
        P("wide", "head"),
        P(None, "wide", None, "head"),
        P("wide", None),
        P("wide"),
        P("wide"),
        P(("wide", "head"), None),
        P(),
        P("wide", None, None, None),
        P("wide", None, None, None),
        P("wide", None),
        P("wide", None),
        P("wide", None),
        P("wide", None, None, None),
        P("wide", None),
        P("wide", None),
    )
    return jax.shard_map(
        per_device, mesh=mesh, in_specs=placed, out_specs=P(("wide", "head"), None), check_vma=False
    )
```

```python
import functools
import math

import jax
import jax.numpy as jnp
from jax import lax
from jax.experimental import pallas as pl
from jax.experimental.pallas import tpu as pltpu
from jax.sharding import PartitionSpec as P

HD = 128
BLK = 128
DEAD = -1e30
MIB = 1024 * 1024

VMEM = pl.BlockSpec(memory_space=pltpu.VMEM)
SMEM = pl.BlockSpec(memory_space=pltpu.SMEM)
HBM = pl.BlockSpec(memory_space=pltpu.HBM)


def copies(pairs, sems):
    return [
        pltpu.make_async_copy(source, target, sems.at[i])
        for i, (source, target) in enumerate(pairs)
    ]


def prepare_kernel(count, *refs):
    page_hbm, length_hbm, sources = refs[0], refs[1], refs[2 : 2 + count]
    targets = refs[2 + count : 2 + 2 * count]
    bias_ref, page_ref, length_ref, sems = refs[2 + 2 * count :]
    spots = bias_ref.shape[1]
    page = spots // sources[0].shape[1]
    lists = copies(((page_hbm, page_ref), (length_hbm, length_ref)), sems.at[pl.ds(0, 2)])
    moves = copies(
        [(s if s.shape == t.shape else s.at[pl.ds(0, t.shape[0])], t) for s, t in zip(sources, targets)],
        sems.at[pl.ds(2, count)],
    )
    for move in lists + moves:
        move.start()
    for move in lists:
        move.wait()
    spot = lax.broadcasted_iota(jnp.int32, (1, spots), 1)
    page_of, offset = spot // page, spot % page
    for r in range(bias_ref.shape[0]):
        place = jnp.full((1, spots), 1 << 20, jnp.int32)
        for i in range(page_ref.shape[1]):
            place = jnp.where(page_of == page_ref[r, i], i * page, place)
        bias_ref[r : r + 1, :] = jnp.where(place + offset < length_ref[r], 0.0, DEAD)
    for move in moves:
        move.wait()


def attend_kernel(groups, per_group, skip, own_ref, next_ref, pool_ref, bias_ref, *refs):
    extra = (len(refs) - 6) // 2
    sources, targets = refs[:extra], refs[extra + 4 : 2 * extra + 4]
    stay_ref, cross_ref, ahead_ref, ahead_cross_ref = refs[extra : extra + 4]
    mixed, sems = refs[-2:]
    moves = copies([(s.at[pl.ds(skip, t.shape[0])], t) for s, t in zip(sources, targets)], sems)
    for move in moves:
        move.start()
    rows = own_ref.shape[0]
    width = groups * per_group * HD
    kv_width = groups * HD
    spots = bias_ref.shape[1]
    head = lax.axis_index("head")

    both = jnp.concatenate(
        [own_ref[...].astype(jnp.float32), next_ref[...].astype(jnp.float32)], axis=0
    )
    shift = lax.broadcasted_iota(jnp.int32, (2 * rows, 1), 0) // rows * rows
    parent = both[:, width + 2 * kv_width : width + 2 * kv_width + 1] + shift.astype(jnp.float32)
    bias = jnp.full((2 * rows, spots), DEAD, jnp.float32)
    for r in range(rows):
        bias = jnp.where(parent == r, bias_ref[r : r + 1, :], bias)
    here = (parent >= 0) & (parent < rows)

    factor = 1.0 / math.sqrt(HD)
    for g in range(groups):
        base = g * per_group * HD
        query = jnp.concatenate(
            [both[:, base + j * HD : base + (j + 1) * HD] for j in range(per_group)], axis=0
        )
        key_own = both[:, width + g * HD : width + (g + 1) * HD]
        value_own = both[:, width + kv_width + g * HD : width + kv_width + (g + 1) * HD]
        keys = pool_ref[0, :, :, g * HD : (g + 1) * HD].reshape(spots, HD)
        values = pool_ref[1, :, :, g * HD : (g + 1) * HD].reshape(spots, HD)
        scores = lax.dot_general(
            query.astype(jnp.bfloat16), keys, (((1,), (1,)), ((), ())),
            preferred_element_type=jnp.float32,
        )
        scores = scores.reshape(per_group, 2 * rows, spots) * factor + bias[None]
        query = query.reshape(per_group, 2 * rows, HD)
        own = jnp.sum(query * key_own[None], axis=-1, keepdims=True) * factor
        top = jnp.maximum(jnp.max(scores, axis=-1, keepdims=True), own)
        expo = jnp.exp(scores - top)
        own_expo = jnp.exp(own - top)
        total = jnp.sum(expo, axis=-1, keepdims=True) + own_expo
        weights = (expo / total).astype(jnp.bfloat16)
        own_weight = (own_expo / total).astype(jnp.bfloat16).astype(jnp.float32)
        mixture = jnp.dot(
            weights.reshape(per_group * 2 * rows, spots), values,
            preferred_element_type=jnp.float32,
        )
        mixture = mixture.reshape(per_group, 2 * rows, HD) + own_weight * value_own[None]
        for j in range(per_group):
            mixed[:, base + j * HD : base + (j + 1) * HD] = jnp.where(here, mixture[j], 0.0)

    part = stay_ref.shape[0]
    for start, mine_ref, other_ref in ((0, stay_ref, cross_ref), (rows, ahead_ref, ahead_cross_ref)):
        low = mixed[start : start + part, :]
        high = mixed[start + part : start + 2 * part, :]
        mine_ref[...] = jnp.where(head == 0, low, high).astype(jnp.bfloat16)
        other_ref[...] = jnp.where(head == 0, high, low).astype(jnp.bfloat16)
    for move in moves:
        move.wait()


def norm_kernel(
    stay_ref, cross_ref, behind_ref, behind_cross_ref, residual_ref, gain_ref,
    middle_ref, normed_ref,
):
    head = lax.axis_index("head")
    half = stay_ref.shape[1]
    f32 = jnp.float32
    same = stay_ref[...].astype(f32) + behind_ref[...].astype(f32)
    other = cross_ref[...].astype(f32) + behind_cross_ref[...].astype(f32)
    first = jnp.where(head == 0, same, other)
    second = jnp.where(head == 0, other, same)
    low = residual_ref[:, :half].astype(f32) + first
    high = residual_ref[:, half:].astype(f32) + second
    middle_ref[:, :half] = low
    middle_ref[:, half:] = high
    square = jnp.sum(low * low, axis=-1, keepdims=True)
    square = square + jnp.sum(high * high, axis=-1, keepdims=True)
    scale = lax.rsqrt(square / (2 * half) + 1e-05)
    normed_ref[:, :half] = (low * scale * gain_ref[:, :half]).astype(jnp.bfloat16)
    normed_ref[:, half:] = (high * scale * gain_ref[:, half:]).astype(jnp.bfloat16)


def feed_kernel(
    brought, keep_ref, gate_scale_ref, up_scale_ref, down_keep_ref, down_scale_ref,
    near_ref, far_ref, gate_hbm, up_hbm, down_hbm, *refs,
):
    columns, keep = keep_ref.shape
    half = near_ref.shape[0]
    stay_ref, send_ref, gate_rest, up_rest, down, hidden, total, sems = refs[-8:]
    pieces = refs[:-8]
    gates, ups = [], []
    for gate_piece, up_piece in zip(pieces[0::2], pieces[1::2]):
        gates += [gate_piece.at[i] for i in range(gate_piece.shape[0])]
        ups += [up_piece.at[i] for i in range(up_piece.shape[0])]
    rest = columns - brought
    gates += [gate_rest.at[i] for i in range(rest)]
    ups += [up_rest.at[i] for i in range(rest)]
    gate_moves = copies([(gate_hbm.at[brought + i], gate_rest.at[i]) for i in range(rest)], sems.at[0])
    up_moves = copies([(up_hbm.at[brought + i], up_rest.at[i]) for i in range(rest)], sems.at[1])
    down_moves = copies([(down_hbm.at[i], down.at[i]) for i in range(columns)], sems.at[2])
    for gate_move, up_move in zip(gate_moves, up_moves):
        gate_move.start()
        up_move.start()
    for move in down_moves:
        move.start()
    total[...] = jnp.zeros_like(total)

    for c in range(columns):
        if c >= brought:
            gate_moves[c - brought].wait()
            up_moves[c - brought].wait()
        gate_sum = jnp.zeros((2 * half, BLK), jnp.float32)
        up_sum = jnp.zeros((2 * half, BLK), jnp.float32)
        for k in range(keep):
            where = pl.ds(pl.multiple_of(keep_ref[c, k] * BLK, BLK), BLK)
            picked = jnp.concatenate([near_ref[:, where], far_ref[:, where]], axis=0)
            both = jnp.dot(
                picked, jnp.concatenate([gates[c][k], ups[c][k]], axis=1),
                preferred_element_type=jnp.float32,
            )
            gate_sum += gate_scale_ref[c, k] * both[:, :BLK]
            up_sum += up_scale_ref[c, k] * both[:, BLK:]
        hidden[c] = (gate_sum / (1.0 + jnp.exp(-gate_sum)) * up_sum).astype(jnp.bfloat16)
    for c in range(columns):
        down_moves[c].wait()
        for k in range(0, keep, 2):
            both = jnp.dot(
                hidden[c], jnp.concatenate([down[c, k], down[c, k + 1]], axis=1),
                preferred_element_type=jnp.float32,
            )
            for j in range(2):
                where = pl.ds(pl.multiple_of(down_keep_ref[c, k + j] * BLK, BLK), BLK)
                total[:, where] += down_scale_ref[c, k + j] * both[:, j * BLK : (j + 1) * BLK]
    stay_ref[...] = total[:half, :]
    send_ref[...] = total[half:, :].astype(jnp.bfloat16)


def in_hbm(arrays):
    return [pltpu.with_memory_space_constraint(a, pltpu.HBM) for a in arrays]


def swapped(block, bit):
    return lax.ppermute(block, "wide", [(i, i ^ bit) for i in range(lax.axis_size("wide"))])


def per_device(
    branch_query, key_new, value_new, pool_pages, page_table, tail_length, parent_row, residual,
    norm_gain, gate_blocks, up_blocks, gate_up_keep, gate_scale, up_scale, down_blocks, down_keep,
    down_scale,
):
    bf16, f32 = jnp.bfloat16, jnp.float32
    wide, heads = lax.axis_size("wide"), lax.axis_size("head")
    rows, width = branch_query.shape
    groups = key_new.shape[1] // HD
    per_group = width // (groups * HD)
    part = residual.shape[0]
    model = residual.shape[1]

    relative = (parent_row - lax.axis_index("wide") * rows).astype(bf16)
    own = jnp.concatenate(
        [branch_query, key_new, value_new, jnp.broadcast_to(relative[:, None], (rows, HD))], axis=1
    )
    following = lax.ppermute(own, "wide", [(i, i - 1) for i in range(1, wide)])
    gain = norm_gain.reshape(1, model)
    columns = gate_blocks.shape[0]
    quarter = columns // 4
    portion = [jax.ShapeDtypeStruct((quarter, *gate_blocks.shape[1:]), bf16)] * (2 if quarter else 0)
    stored = [pool_pages, residual, gain, gate_up_keep, gate_scale, up_scale, down_keep, down_scale]
    shapes = [jax.ShapeDtypeStruct(a.shape, a.dtype) for a in stored] + portion
    moved = stored + [gate_blocks, up_blocks][: len(portion)]
    spots = pool_pages.shape[1] * pool_pages.shape[2]
    prepared = pl.pallas_call(
        functools.partial(prepare_kernel, len(moved)),
        out_shape=(*shapes, jax.ShapeDtypeStruct((rows, spots), f32)),
        in_specs=[HBM] * (2 + len(moved)),
        out_specs=(VMEM,) * (len(moved) + 1),
        scratch_shapes=[
            pltpu.SMEM(page_table.shape, jnp.int32),
            pltpu.SMEM(tail_length.shape, jnp.int32),
            pltpu.SemaphoreType.DMA((2 + len(moved),)),
        ],
        compiler_params=pltpu.CompilerParams(vmem_limit_bytes=4 * MIB),
        cost_estimate=pl.CostEstimate(flops=0, bytes_accessed=8 * MIB, transcendentals=0),
        name="prepare",
    )(*in_hbm([page_table, tail_length, *moved]))
    pool, residual, gain, *lists = prepared[: len(stored)]
    pieces = list(prepared[len(stored) : -1])
    bias = prepared[-1]

    piece = jax.ShapeDtypeStruct((part, width), bf16)
    stay, cross, ahead, ahead_cross, *more = pl.pallas_call(
        functools.partial(attend_kernel, groups, per_group, quarter),
        out_shape=(*(piece,) * 4, *portion),
        in_specs=[VMEM] * 4 + [HBM] * len(portion),
        out_specs=(VMEM,) * (4 + len(portion)),
        scratch_shapes=[
            pltpu.VMEM((2 * rows, width), f32),
            pltpu.SemaphoreType.DMA((max(len(portion), 1),)),
        ],
        compiler_params=pltpu.CompilerParams(vmem_limit_bytes=8 * MIB),
        name="attend",
    )(own, following, pool, bias, *in_hbm([gate_blocks, up_blocks][: len(portion)]))
    pieces += more

    cross = lax.ppermute(cross, "head", [(h, 1 - h) for h in range(heads)])
    behind = lax.ppermute(ahead, "wide", [(i, i + 1) for i in range(wide - 1)])
    behind_cross = lax.ppermute(
        ahead_cross,
        ("wide", "head"),
        [(i * heads + h, (i + 1) * heads + 1 - h) for i in range(wide - 1) for h in range(heads)],
    )
    middle, normed = pl.pallas_call(
        norm_kernel,
        out_shape=(
            jax.ShapeDtypeStruct((part, model), f32),
            jax.ShapeDtypeStruct((part, model), bf16),
        ),
        in_specs=[VMEM] * 6,
        out_specs=(VMEM,) * 2,
        compiler_params=pltpu.CompilerParams(vmem_limit_bytes=8 * MIB),
        name="norm",
    )(stay, cross, behind, behind_cross, residual, gain)

    bits = [1 << b for b in range(wide.bit_length() - 1)]
    gathered = normed
    for bit in bits[:0:-1]:
        gathered = jnp.concatenate([gathered, swapped(gathered, bit)], axis=0)
    far = swapped(gathered, bits[0])

    half = gathered.shape[0]
    rest = jax.ShapeDtypeStruct((columns - 2 * quarter, *gate_blocks.shape[1:]), bf16)
    size = 2 * half * model * 4 + half * model * 10 + 2 * (2 * rest.size + down_blocks.size)
    kept, sent = pl.pallas_call(
        functools.partial(feed_kernel, 2 * quarter),
        out_shape=(
            jax.ShapeDtypeStruct((half, model), f32),
            jax.ShapeDtypeStruct((half, model), bf16),
        ),
        in_specs=[SMEM] * 5 + [VMEM] * 2 + [HBM] * 3 + [VMEM] * len(pieces),
        out_specs=(VMEM,) * 2,
        scratch_shapes=[
            pltpu.VMEM(rest.shape, bf16),
            pltpu.VMEM(rest.shape, bf16),
            pltpu.VMEM(down_blocks.shape, bf16),
            pltpu.VMEM((columns, 2 * half, BLK), bf16),
            pltpu.VMEM((2 * half, model), f32),
            pltpu.SemaphoreType.DMA((3, columns)),
        ],
        compiler_params=pltpu.CompilerParams(vmem_limit_bytes=size + 4 * MIB),
        name="feed",
    )(*lists, gathered, far, *in_hbm([gate_blocks, up_blocks, down_blocks]), *pieces)

    for bit in bits:
        summed = kept + swapped(sent, bit).astype(f32)
        if bit != bits[-1]:
            half = half // 2
            kept, sent = summed[:half], summed[half:].astype(bf16)
    return (middle + summed).astype(bf16)


def solution(mesh):
    placed = (
        P("wide", "head"),
        P("wide", "head"),
        P("wide", "head"),
        P(None, "wide", None, "head"),
        P("wide", None),
        P("wide"),
        P("wide"),
        P(("wide", "head"), None),
        P(),
        P("wide", None, None, None),
        P("wide", None, None, None),
        P("wide", None),
        P("wide", None),
        P("wide", None),
        P("wide", None, None, None),
        P("wide", None),
        P("wide", None),
    )
    return jax.shard_map(
        per_device, mesh=mesh, in_specs=placed, out_specs=P(("wide", "head"), None), check_vma=False
    )
```

```python
import functools
import math

import jax
import jax.numpy as jnp
from jax import lax
from jax.experimental import pallas as pl
from jax.experimental.pallas import tpu as pltpu
from jax.sharding import PartitionSpec as P

HD = 128
BLK = 128
TILE = 8
DEAD = -1e30
MIB = 1024 * 1024

VMEM = pl.BlockSpec(memory_space=pltpu.VMEM)
SMEM = pl.BlockSpec(memory_space=pltpu.SMEM)
HBM = pl.BlockSpec(memory_space=pltpu.HBM)


def in_hbm(arrays):
    return [pltpu.with_memory_space_constraint(a, pltpu.HBM) for a in arrays]


def like(array):
    return jax.ShapeDtypeStruct(array.shape, array.dtype)


def copies(pairs, sems):
    return [
        pltpu.make_async_copy(source, target, sems.at[i])
        for i, (source, target) in enumerate(pairs)
    ]


def pack_kernel(query_hbm, key_hbm, value_hbm, parent_hbm, packed_ref, parent_ref, sems):
    rows, width = query_hbm.shape
    kv_width = key_hbm.shape[1]
    moves = copies(
        (
            (parent_hbm, parent_ref),
            (query_hbm, packed_ref.at[:, pl.ds(0, width)]),
            (key_hbm, packed_ref.at[:, pl.ds(width, kv_width)]),
            (value_hbm, packed_ref.at[:, pl.ds(width + kv_width, kv_width)]),
        ),
        sems,
    )
    for move in moves:
        move.start()
    moves[0].wait()
    first = lax.axis_index("wide") * rows
    row = lax.broadcasted_iota(jnp.int32, (rows, HD), 0)
    parent = jnp.zeros((rows, HD), jnp.int32)
    for r in range(rows):
        parent = jnp.where(row == r, parent_ref[r] - first, parent)
    packed_ref[:, width + 2 * kv_width :] = parent.astype(jnp.float32).astype(jnp.bfloat16)
    for move in moves[1:]:
        move.wait()


def attend_kernel(groups, per_group, shift, packed_ref, pool_ref, bias_ref, *refs):
    out_ref = refs[-1]
    rows = packed_ref.shape[0]
    width = groups * per_group * HD
    kv_width = groups * HD
    spots = bias_ref.shape[1]
    fold = TILE // rows

    def tiled(block):
        return jnp.concatenate([block] * fold, axis=0)

    packed = packed_ref[...].astype(jnp.float32)
    parent = packed[:, width + 2 * kv_width : width + 2 * kv_width + 1] + shift
    bias = jnp.full((rows, spots), DEAD, jnp.float32)
    for r in range(rows):
        bias = jnp.where(parent == r, bias_ref[r : r + 1, :], bias)
    bias = tiled(bias)
    here = (parent >= 0) & (parent < rows)

    factor = 1.0 / math.sqrt(HD)
    for g in range(groups):
        base = g * per_group * HD
        query = jnp.concatenate(
            [packed[:, base + j * HD : base + (j + 1) * HD] for j in range(per_group)], axis=0
        )
        key_own = tiled(packed[:, width + g * HD : width + (g + 1) * HD])
        value_own = tiled(packed[:, width + kv_width + g * HD : width + kv_width + (g + 1) * HD])
        keys = pool_ref[0, :, :, g * HD : (g + 1) * HD].reshape(spots, HD)
        values = pool_ref[1, :, :, g * HD : (g + 1) * HD].reshape(spots, HD)
        scores = lax.dot_general(
            query.astype(jnp.bfloat16), keys, (((1,), (1,)), ((), ())),
            preferred_element_type=jnp.float32,
        )
        scores = scores.reshape(-1, TILE, spots) * factor + bias[None]
        query = query.reshape(-1, TILE, HD)
        own = jnp.sum(query * key_own[None], axis=-1, keepdims=True) * factor
        top = jnp.maximum(jnp.max(scores, axis=-1, keepdims=True), own)
        expo = jnp.exp(scores - top)
        own_expo = jnp.exp(own - top)
        total = jnp.sum(expo, axis=-1, keepdims=True) + own_expo
        weights = (expo / total).astype(jnp.bfloat16)
        own_weight = (own_expo / total).astype(jnp.bfloat16).astype(jnp.float32)
        mixture = jnp.dot(
            weights.reshape(per_group * rows, spots), values, preferred_element_type=jnp.float32
        )
        mixture = mixture.reshape(-1, TILE, HD) + own_weight * value_own[None]
        mixture = mixture.reshape(per_group * rows, HD)
        for j in range(per_group):
            out_ref[:, base + j * HD : base + (j + 1) * HD] = jnp.where(
                here, mixture[j * rows : (j + 1) * rows], 0.0
            ).astype(jnp.bfloat16)


def prepare_kernel(count, *refs):
    page_hbm, length_hbm, sources = refs[0], refs[1], refs[2 : 2 + count]
    bias_ref, targets = refs[2 + count], refs[3 + count : 3 + 2 * count]
    page_ref, length_ref, sems = refs[3 + 2 * count :]
    moves = copies(
        ((page_hbm, page_ref), (length_hbm, length_ref), *zip(sources, targets)), sems
    )
    for move in moves:
        move.start()
    moves[0].wait()
    moves[1].wait()
    spots = bias_ref.shape[1]
    page = spots // sources[0].shape[1]
    spot = lax.broadcasted_iota(jnp.int32, (1, spots), 1)
    page_of, offset = spot // page, spot % page
    for r in range(bias_ref.shape[0]):
        place = jnp.full((1, spots), 1 << 20, jnp.int32)
        for i in range(page_ref.shape[1]):
            place = jnp.where(page_of == page_ref[r, i], i * page, place)
        bias_ref[r : r + 1, :] = jnp.where(place + offset < length_ref[r], 0.0, DEAD)
    for move in moves[2:]:
        move.wait()


def load_kernel(skip, after_ref, gate_hbm, up_hbm, token_ref, gate_ref, up_ref, sems):
    del after_ref
    moves = copies(
        [
            (source.at[pl.ds(skip, target.shape[0])], target)
            for source, target in ((gate_hbm, gate_ref), (up_hbm, up_ref))
        ],
        sems,
    )
    for move in moves:
        move.start()
    token_ref[...] = jnp.zeros_like(token_ref)
    for move in moves:
        move.wait()


def merge_kernel(own_ref, behind_ref, *refs):
    stay_ref, cross_ref = refs[-2:]
    head = lax.axis_index("head")
    part = stay_ref.shape[0]
    both = own_ref[...].astype(jnp.float32) + behind_ref[...].astype(jnp.float32)
    low, high = both[:part], both[part : 2 * part]
    stay_ref[...] = jnp.where(head == 0, low, high).astype(jnp.bfloat16)
    cross_ref[...] = jnp.where(head == 0, high, low).astype(jnp.bfloat16)


def norm_kernel(stay_ref, cross_ref, residual_ref, gain_ref, *refs):
    middle_ref, normed_ref = refs[-2:]
    head = lax.axis_index("head")
    half = stay_ref.shape[1]
    f32 = jnp.float32
    same, other = stay_ref[...].astype(f32), cross_ref[...].astype(f32)
    low = residual_ref[:, :half].astype(f32) + jnp.where(head == 0, same, other)
    high = residual_ref[:, half:].astype(f32) + jnp.where(head == 0, other, same)
    middle_ref[:, :half] = low
    middle_ref[:, half:] = high
    square = jnp.sum(low * low, axis=-1, keepdims=True)
    square = square + jnp.sum(high * high, axis=-1, keepdims=True)
    scale = lax.rsqrt(square / (2 * half) + 1e-05)
    normed_ref[:, :half] = (low * scale * gain_ref[:, :half]).astype(jnp.bfloat16)
    normed_ref[:, half:] = (high * scale * gain_ref[:, half:]).astype(jnp.bfloat16)


def feed_kernel(
    brought, keep_ref, gate_scale_ref, up_scale_ref, down_keep_ref, down_scale_ref,
    near_ref, far_ref, gate_hbm, up_hbm, down_hbm, *refs,
):
    columns, keep = keep_ref.shape
    half = near_ref.shape[0]
    rest = columns - brought
    stay_ref, send_ref, gate_rest, up_rest, down, hidden, total, sems = refs[-8:]
    gates, ups = [], []
    pieces = refs[: 2 if brought else 0]
    for gate_piece, up_piece in zip(pieces[0::2], pieces[1::2]):
        gates += [gate_piece.at[i] for i in range(gate_piece.shape[0])]
        ups += [up_piece.at[i] for i in range(up_piece.shape[0])]
    gates += [gate_rest.at[i] for i in range(rest)]
    ups += [up_rest.at[i] for i in range(rest)]
    moves = copies(
        (
            (gate_hbm.at[pl.ds(brought, rest)], gate_rest),
            (up_hbm.at[pl.ds(brought, rest)], up_rest),
        ),
        sems.at[0],
    )
    late = columns // 4
    ends = [0, columns - late, columns] if late else [0, columns]
    down_moves = copies(
        [
            (down_hbm.at[pl.ds(start, end - start)], down.at[pl.ds(start, end - start)])
            for start, end in zip(ends, ends[1:])
        ],
        sems.at[1],
    )
    for move in moves + down_moves:
        move.start()
    total[...] = jnp.zeros_like(total)

    for c in range(columns):
        if c == brought:
            for move in moves:
                move.wait()
        gate_sum = jnp.zeros((2 * half, BLK), jnp.float32)
        up_sum = jnp.zeros((2 * half, BLK), jnp.float32)
        for k in range(keep):
            where = pl.ds(pl.multiple_of(keep_ref[c, k] * BLK, BLK), BLK)
            picked = jnp.concatenate([near_ref[:, where], far_ref[:, where]], axis=0)
            both = jnp.dot(
                picked, jnp.concatenate([gates[c][k], ups[c][k]], axis=1),
                preferred_element_type=jnp.float32,
            )
            gate_sum += gate_scale_ref[c, k] * both[:, :BLK]
            up_sum += up_scale_ref[c, k] * both[:, BLK:]
        hidden[c] = (gate_sum / (1.0 + jnp.exp(-gate_sum)) * up_sum).astype(jnp.bfloat16)
    for c in range(columns):
        if c in ends:
            down_moves[ends.index(c)].wait()
        for k in range(0, keep, 2):
            both = jnp.dot(
                hidden[c], jnp.concatenate([down[c, k], down[c, k + 1]], axis=1),
                preferred_element_type=jnp.float32,
            )
            for j in range(2):
                where = pl.ds(pl.multiple_of(down_keep_ref[c, k + j] * BLK, BLK), BLK)
                total[:, where] += down_scale_ref[c, k + j] * both[:, j * BLK : (j + 1) * BLK]
    stay_ref[...] = total[:half, :]
    send_ref[...] = total[half:, :].astype(jnp.bfloat16)


def join_kernel(count, *refs):
    out_ref = refs[-1]
    height = refs[0].shape[0]
    for i, ref in enumerate(refs[:count]):
        out_ref[i * height : (i + 1) * height, :] = ref[...]


def joined(blocks, tokens):
    height, width = blocks[0].shape
    return pl.pallas_call(
        functools.partial(join_kernel, len(blocks)),
        out_shape=jax.ShapeDtypeStruct((len(blocks) * height, width), blocks[0].dtype),
        in_specs=[VMEM] * (len(blocks) + len(tokens)),
        out_specs=VMEM,
        compiler_params=pltpu.CompilerParams(vmem_limit_bytes=2 * MIB),
        name="join",
    )(*blocks, *tokens)


def swapped(block, bits):
    return lax.ppermute(block, "wide", [(i, i ^ bits) for i in range(lax.axis_size("wide"))])


def combined(bits):
    sums = [0]
    for bit in bits:
        sums += [s + bit for s in sums]
    return sums[1:]


def per_device(
    branch_query, key_new, value_new, pool_pages, page_table, tail_length, parent_row, residual,
    norm_gain, gate_blocks, up_blocks, gate_up_keep, gate_scale, up_scale, down_blocks, down_keep,
    down_scale,
):
    bf16, f32 = jnp.bfloat16, jnp.float32
    wide, heads = lax.axis_size("wide"), lax.axis_size("head")
    rows, width = branch_query.shape
    kv_width = key_new.shape[1]
    groups = kv_width // HD
    per_group = width // kv_width
    part, model = residual.shape
    columns = gate_blocks.shape[0]

    own = pl.pallas_call(
        pack_kernel,
        out_shape=jax.ShapeDtypeStruct((rows, width + 2 * kv_width + HD), bf16),
        in_specs=[HBM] * 4,
        out_specs=VMEM,
        scratch_shapes=[
            pltpu.SMEM(parent_row.shape, jnp.int32),
            pltpu.SemaphoreType.DMA((4,)),
        ],
        compiler_params=pltpu.CompilerParams(vmem_limit_bytes=2 * MIB),
        name="pack",
    )(*in_hbm([branch_query, key_new, value_new, parent_row]))
    following = lax.ppermute(own, "wide", [(i, i - 1) for i in range(1, wide)])

    stored = [pool_pages, residual, norm_gain.reshape(1, model)]
    stored += [gate_up_keep, gate_scale, up_scale, down_keep, down_scale]
    spots = pool_pages.shape[1] * pool_pages.shape[2]
    bias, pool, residual, gain, *lists = pl.pallas_call(
        functools.partial(prepare_kernel, len(stored)),
        out_shape=(jax.ShapeDtypeStruct((rows, spots), f32), *[like(a) for a in stored]),
        in_specs=[HBM] * (2 + len(stored)),
        out_specs=(VMEM,) * (1 + len(stored)),
        scratch_shapes=[
            pltpu.SMEM(page_table.shape, jnp.int32),
            pltpu.SMEM(tail_length.shape, jnp.int32),
            pltpu.SemaphoreType.DMA((2 + len(stored),)),
        ],
        compiler_params=pltpu.CompilerParams(vmem_limit_bytes=2 * MIB),
        cost_estimate=pl.CostEstimate(flops=0, bytes_accessed=8 * MIB, transcendentals=0),
        name="prepare",
    )(*in_hbm([page_table, tail_length, *stored]))

    def attended(packed, shift, *after):
        return pl.pallas_call(
            functools.partial(attend_kernel, groups, per_group, shift),
            out_shape=jax.ShapeDtypeStruct((rows, width), bf16),
            in_specs=[VMEM] * (3 + len(after)),
            out_specs=VMEM,
            compiler_params=pltpu.CompilerParams(vmem_limit_bytes=6 * MIB),
            name="attend",
        )(packed, pool, bias, *after)

    ahead = attended(following, rows)
    behind = lax.ppermute(ahead, "wide", [(i, i + 1) for i in range(wide - 1)])
    mixed = attended(own, 0, ahead)
    per_load = columns // 2
    portion = pltpu.VMEM((per_load, *gate_blocks.shape[1:]), bf16)
    pieces = []

    def load(after):
        if not per_load:
            return []
        token, gate_piece, up_piece = pl.pallas_call(
            functools.partial(load_kernel, len(pieces) // 2 * per_load),
            out_shape=(jax.ShapeDtypeStruct((8, HD), f32), portion, portion),
            in_specs=[VMEM, HBM, HBM],
            out_specs=(VMEM,) * 3,
            scratch_shapes=[pltpu.SemaphoreType.DMA((2,))],
            compiler_params=pltpu.CompilerParams(vmem_limit_bytes=2 * MIB),
            cost_estimate=pl.CostEstimate(
                flops=0, bytes_accessed=4 * gate_blocks.size // 2, transcendentals=0
            ),
            name="load",
        )(after, *in_hbm([gate_blocks, up_blocks]))
        pieces.extend([gate_piece, up_piece])
        return [token]

    stay, cross = pl.pallas_call(
        merge_kernel,
        out_shape=(jax.ShapeDtypeStruct((part, width), bf16),) * 2,
        in_specs=[VMEM] * 2,
        out_specs=(VMEM,) * 2,
        compiler_params=pltpu.CompilerParams(vmem_limit_bytes=2 * MIB),
        name="merge",
    )(mixed, behind)
    crossed = lax.ppermute(cross, "head", [(h, 1 - h) for h in range(heads)])
    middle, normed = pl.pallas_call(
        norm_kernel,
        out_shape=(
            jax.ShapeDtypeStruct((part, model), f32),
            jax.ShapeDtypeStruct((part, model), bf16),
        ),
        in_specs=[VMEM] * 4,
        out_specs=(VMEM,) * 2,
        compiler_params=pltpu.CompilerParams(vmem_limit_bytes=2 * MIB),
        name="norm",
    )(stay, crossed, residual, gain)

    bits = [1 << b for b in range(wide.bit_length() - 1)]
    stages = [(bits[0],), tuple(bits[1:3]), *[(bit,) for bit in bits[3:]]]
    gathered = normed
    for stage in stages[:0:-1]:
        blocks = [gathered] + [swapped(gathered, s) for s in combined(stage)]
        tokens = load(gathered) if len(stage) > 1 else []
        gathered = joined(blocks, tokens)
    far = swapped(gathered, bits[0])

    half = gathered.shape[0]
    rest = columns - len(pieces) // 2 * per_load
    kept_back = [pltpu.VMEM((rest, *gate_blocks.shape[1:]), bf16)] * 2
    size = 2 * half * model * 4 + half * model * 6 + 2 * down_blocks.size
    size += 4 * rest * gate_blocks.size // columns
    kept, sent = pl.pallas_call(
        functools.partial(feed_kernel, columns - rest),
        out_shape=(
            jax.ShapeDtypeStruct((half, model), f32),
            jax.ShapeDtypeStruct((half, model), bf16),
        ),
        in_specs=[SMEM] * 5 + [VMEM] * 2 + [HBM] * 3 + [VMEM] * len(pieces),
        out_specs=(VMEM,) * 2,
        scratch_shapes=kept_back
        + [
            pltpu.VMEM(down_blocks.shape, bf16),
            pltpu.VMEM((columns, 2 * half, BLK), bf16),
            pltpu.VMEM((2 * half, model), f32),
            pltpu.SemaphoreType.DMA((2, 2)),
        ],
        compiler_params=pltpu.CompilerParams(vmem_limit_bytes=size + 4 * MIB),
        name="feed",
    )(*lists, gathered, far, *in_hbm([gate_blocks, up_blocks, down_blocks]), *pieces)

    total = kept + swapped(sent, bits[0]).astype(f32)
    for stage in stages[1:]:
        half = half >> len(stage)
        kept, sent = total[:half], total[half:].astype(bf16)
        total = kept
        for i, s in enumerate(combined(stage)):
            total = total + swapped(sent[i * half : (i + 1) * half], s).astype(f32)
    return (middle + total).astype(bf16)


def solution(mesh):
    placed = (
        P("wide", "head"),
        P("wide", "head"),
        P("wide", "head"),
        P(None, "wide", None, "head"),
        P("wide", None),
        P("wide"),
        P("wide"),
        P(("wide", "head"), None),
        P(),
        P("wide", None, None, None),
        P("wide", None, None, None),
        P("wide", None),
        P("wide", None),
        P("wide", None),
        P("wide", None, None, None),
        P("wide", None),
        P("wide", None),
    )
    return jax.shard_map(
        per_device, mesh=mesh, in_specs=placed, out_specs=P(("wide", "head"), None), check_vma=False
    )
```

```python
import functools
import math

import jax
import jax.numpy as jnp
from jax import lax
from jax.experimental import pallas as pl
from jax.experimental.pallas import tpu as pltpu
from jax.sharding import PartitionSpec as P

HD = 128
BLK = 128
TILE = 8
DEAD = -1e30
MIB = 1024 * 1024
WHILE_EXCHANGING = pl.CostEstimate(flops=20 * 10**9, bytes_accessed=64 * MIB, transcendentals=0)

VMEM = pl.BlockSpec(memory_space=pltpu.VMEM)
SMEM = pl.BlockSpec(memory_space=pltpu.SMEM)
HBM = pl.BlockSpec(memory_space=pltpu.HBM)


def in_hbm(arrays):
    return [pltpu.with_memory_space_constraint(a, pltpu.HBM) for a in arrays]


def like(array):
    return jax.ShapeDtypeStruct(array.shape, array.dtype)


def copies(pairs, sems):
    return [
        pltpu.make_async_copy(source, target, sems.at[i])
        for i, (source, target) in enumerate(pairs)
    ]


def pack_kernel(query_hbm, key_hbm, value_hbm, parent_hbm, packed_ref, parent_ref, sems):
    rows, width = query_hbm.shape
    kv_width = key_hbm.shape[1]
    moves = copies(
        (
            (parent_hbm, parent_ref),
            (query_hbm, packed_ref.at[:, pl.ds(0, width)]),
            (key_hbm, packed_ref.at[:, pl.ds(width, kv_width)]),
            (value_hbm, packed_ref.at[:, pl.ds(width + kv_width, kv_width)]),
        ),
        sems,
    )
    for move in moves:
        move.start()
    moves[0].wait()
    first = lax.axis_index("wide") * rows
    row = lax.broadcasted_iota(jnp.int32, (rows, HD), 0)
    parent = jnp.zeros((rows, HD), jnp.int32)
    for r in range(rows):
        parent = jnp.where(row == r, parent_ref[r] - first, parent)
    packed_ref[:, width + 2 * kv_width :] = parent.astype(jnp.float32).astype(jnp.bfloat16)
    for move in moves[1:]:
        move.wait()


def attend_kernel(groups, per_group, shift, packed_ref, pool_ref, bias_ref, *refs):
    out_ref = refs[-1]
    rows = packed_ref.shape[0]
    width = groups * per_group * HD
    kv_width = groups * HD
    spots = bias_ref.shape[1]
    fold = TILE // rows

    def tiled(block):
        return jnp.concatenate([block] * fold, axis=0)

    packed = packed_ref[...].astype(jnp.float32)
    parent = packed[:, width + 2 * kv_width : width + 2 * kv_width + 1] + shift
    bias = jnp.full((rows, spots), DEAD, jnp.float32)
    for r in range(rows):
        bias = jnp.where(parent == r, bias_ref[r : r + 1, :], bias)
    bias = tiled(bias)
    here = (parent >= 0) & (parent < rows)

    factor = 1.0 / math.sqrt(HD)
    for g in range(groups):
        base = g * per_group * HD
        query = jnp.concatenate(
            [packed[:, base + j * HD : base + (j + 1) * HD] for j in range(per_group)], axis=0
        )
        key_own = tiled(packed[:, width + g * HD : width + (g + 1) * HD])
        value_own = tiled(packed[:, width + kv_width + g * HD : width + kv_width + (g + 1) * HD])
        keys = pool_ref[0, :, :, g * HD : (g + 1) * HD].reshape(spots, HD)
        values = pool_ref[1, :, :, g * HD : (g + 1) * HD].reshape(spots, HD)
        scores = lax.dot_general(
            query.astype(jnp.bfloat16), keys, (((1,), (1,)), ((), ())),
            preferred_element_type=jnp.float32,
        )
        scores = scores.reshape(-1, TILE, spots) * factor + bias[None]
        query = query.reshape(-1, TILE, HD)
        own = jnp.sum(query * key_own[None], axis=-1, keepdims=True) * factor
        top = jnp.maximum(jnp.max(scores, axis=-1, keepdims=True), own)
        expo = jnp.exp(scores - top)
        own_expo = jnp.exp(own - top)
        total = jnp.sum(expo, axis=-1, keepdims=True) + own_expo
        weights = (expo / total).astype(jnp.bfloat16)
        own_weight = (own_expo / total).astype(jnp.bfloat16).astype(jnp.float32)
        mixture = jnp.dot(
            weights.reshape(per_group * rows, spots), values, preferred_element_type=jnp.float32
        )
        mixture = mixture.reshape(-1, TILE, HD) + own_weight * value_own[None]
        mixture = mixture.reshape(per_group * rows, HD)
        for j in range(per_group):
            out_ref[:, base + j * HD : base + (j + 1) * HD] = jnp.where(
                here, mixture[j * rows : (j + 1) * rows], 0.0
            ).astype(jnp.bfloat16)


def prepare_kernel(count, *refs):
    page_hbm, length_hbm, sources = refs[0], refs[1], refs[2 : 2 + count]
    bias_ref, targets = refs[2 + count], refs[3 + count : 3 + 2 * count]
    page_ref, length_ref, sems = refs[3 + 2 * count :]
    moves = copies(
        ((page_hbm, page_ref), (length_hbm, length_ref), *zip(sources, targets)), sems
    )
    for move in moves:
        move.start()
    moves[0].wait()
    moves[1].wait()
    spots = bias_ref.shape[1]
    page = spots // sources[0].shape[1]
    spot = lax.broadcasted_iota(jnp.int32, (1, spots), 1)
    page_of, offset = spot // page, spot % page
    for r in range(bias_ref.shape[0]):
        place = jnp.full((1, spots), 1 << 20, jnp.int32)
        for i in range(page_ref.shape[1]):
            place = jnp.where(page_of == page_ref[r, i], i * page, place)
        bias_ref[r : r + 1, :] = jnp.where(place + offset < length_ref[r], 0.0, DEAD)
    for move in moves[2:]:
        move.wait()


def merge_kernel(own_ref, behind_ref, residual_ref, cross_ref, stay_ref):
    head = lax.axis_index("head")
    part, width = cross_ref.shape
    both = own_ref[...].astype(jnp.float32) + behind_ref[...].astype(jnp.float32)
    low, high = both[:part], both[part : 2 * part]
    cross_ref[...] = jnp.where(head == 0, high, low).astype(jnp.bfloat16)
    stay_ref[:, :width] = jnp.where(head == 0, low, high).astype(jnp.bfloat16)
    stay_ref[:, width:] = residual_ref[...]


def norm_kernel(stay_ref, cross_ref, far_stay_ref, far_cross_ref, gain_ref, middle_ref, normed_ref):
    head = lax.axis_index("head")
    part, half = cross_ref.shape
    f32 = jnp.float32
    for i, (stay, cross) in enumerate(((stay_ref, cross_ref), (far_stay_ref, far_cross_ref))):
        same, other = stay[:, :half].astype(f32), cross[...].astype(f32)
        low = stay[:, half : 2 * half].astype(f32) + jnp.where(head == 0, same, other)
        high = stay[:, 2 * half :].astype(f32) + jnp.where(head == 0, other, same)
        if i == 0:
            middle_ref[:, :half] = low
            middle_ref[:, half:] = high
        square = jnp.sum(low * low, axis=-1, keepdims=True)
        square = square + jnp.sum(high * high, axis=-1, keepdims=True)
        scale = lax.rsqrt(square / (2 * half) + 1e-05)
        rows = slice(i * part, (i + 1) * part)
        normed_ref[rows, :half] = (low * scale * gain_ref[:, :half]).astype(jnp.bfloat16)
        normed_ref[rows, half:] = (high * scale * gain_ref[:, half:]).astype(jnp.bfloat16)


def feed_kernel(
    keep_ref, gate_scale_ref, up_scale_ref, down_keep_ref, down_scale_ref,
    near_ref, far_ref, gate_ref, up_ref, down_ref, stay_ref, send_ref, hidden, total,
):
    columns, keep = keep_ref.shape
    half = near_ref.shape[0]
    total[...] = jnp.zeros_like(total)

    for c in range(columns):
        gate_sum = jnp.zeros((2 * half, BLK), jnp.float32)
        up_sum = jnp.zeros((2 * half, BLK), jnp.float32)
        for k in range(keep):
            where = pl.ds(pl.multiple_of(keep_ref[c, k] * BLK, BLK), BLK)
            picked = jnp.concatenate([near_ref[:, where], far_ref[:, where]], axis=0)
            both = jnp.dot(
                picked, jnp.concatenate([gate_ref[c, k], up_ref[c, k]], axis=1),
                preferred_element_type=jnp.float32,
            )
            gate_sum += gate_scale_ref[c, k] * both[:, :BLK]
            up_sum += up_scale_ref[c, k] * both[:, BLK:]
        hidden[c] = (gate_sum / (1.0 + jnp.exp(-gate_sum)) * up_sum).astype(jnp.bfloat16)
    for c in range(columns):
        for k in range(0, keep, 2):
            both = jnp.dot(
                hidden[c], jnp.concatenate([down_ref[c, k], down_ref[c, k + 1]], axis=1),
                preferred_element_type=jnp.float32,
            )
            for j in range(2):
                where = pl.ds(pl.multiple_of(down_keep_ref[c, k + j] * BLK, BLK), BLK)
                total[:, where] += down_scale_ref[c, k + j] * both[:, j * BLK : (j + 1) * BLK]
    stay_ref[...] = total[:half, :]
    send_ref[...] = total[half:, :].astype(jnp.bfloat16)


def join_kernel(*refs):
    out_ref = refs[-1]
    height = refs[0].shape[0]
    for i, ref in enumerate(refs[:-1]):
        out_ref[i * height : (i + 1) * height, :] = ref[...]


def joined(blocks):
    height, width = blocks[0].shape
    return pl.pallas_call(
        join_kernel,
        out_shape=jax.ShapeDtypeStruct((len(blocks) * height, width), blocks[0].dtype),
        in_specs=[VMEM] * len(blocks),
        out_specs=VMEM,
        compiler_params=pltpu.CompilerParams(vmem_limit_bytes=2 * MIB),
        cost_estimate=WHILE_EXCHANGING,
        name="join",
    )(*blocks)


def swapped(block, bits):
    return lax.ppermute(block, "wide", [(i, i ^ bits) for i in range(lax.axis_size("wide"))])


def combined(bits):
    sums = [0]
    for bit in bits:
        sums += [s + bit for s in sums]
    return sums[1:]


def per_device(
    branch_query, key_new, value_new, pool_pages, page_table, tail_length, parent_row, residual,
    norm_gain, gate_blocks, up_blocks, gate_up_keep, gate_scale, up_scale, down_blocks, down_keep,
    down_scale,
):
    bf16, f32 = jnp.bfloat16, jnp.float32
    wide, heads = lax.axis_size("wide"), lax.axis_size("head")
    rows, width = branch_query.shape
    kv_width = key_new.shape[1]
    groups = kv_width // HD
    per_group = width // kv_width
    part, model = residual.shape
    columns = gate_blocks.shape[0]

    own = pl.pallas_call(
        pack_kernel,
        out_shape=jax.ShapeDtypeStruct((rows, width + 2 * kv_width + HD), bf16),
        in_specs=[HBM] * 4,
        out_specs=VMEM,
        scratch_shapes=[
            pltpu.SMEM(parent_row.shape, jnp.int32),
            pltpu.SemaphoreType.DMA((4,)),
        ],
        compiler_params=pltpu.CompilerParams(vmem_limit_bytes=2 * MIB),
        name="pack",
    )(*in_hbm([branch_query, key_new, value_new, parent_row]))
    following = lax.ppermute(own, "wide", [(i, i - 1) for i in range(1, wide)])

    stored = [pool_pages, residual, norm_gain.reshape(1, model)]
    stored += [gate_up_keep, gate_scale, up_scale, down_keep, down_scale]
    spots = pool_pages.shape[1] * pool_pages.shape[2]
    bias, pool, residual, gain, *lists = pl.pallas_call(
        functools.partial(prepare_kernel, len(stored)),
        out_shape=(jax.ShapeDtypeStruct((rows, spots), f32), *[like(a) for a in stored]),
        in_specs=[HBM] * (2 + len(stored)),
        out_specs=(VMEM,) * (1 + len(stored)),
        scratch_shapes=[
            pltpu.SMEM(page_table.shape, jnp.int32),
            pltpu.SMEM(tail_length.shape, jnp.int32),
            pltpu.SemaphoreType.DMA((2 + len(stored),)),
        ],
        compiler_params=pltpu.CompilerParams(vmem_limit_bytes=2 * MIB),
        cost_estimate=pl.CostEstimate(flops=0, bytes_accessed=8 * MIB, transcendentals=0),
        name="prepare",
    )(*in_hbm([page_table, tail_length, *stored]))

    def attended(packed, shift, *after):
        return pl.pallas_call(
            functools.partial(attend_kernel, groups, per_group, shift),
            out_shape=jax.ShapeDtypeStruct((rows, width), bf16),
            in_specs=[VMEM] * (3 + len(after)),
            out_specs=VMEM,
            compiler_params=pltpu.CompilerParams(vmem_limit_bytes=6 * MIB),
            name="attend",
        )(packed, pool, bias, *after)

    ahead = attended(following, rows)
    behind = lax.ppermute(ahead, "wide", [(i, i + 1) for i in range(wide - 1)])
    mixed = attended(own, 0, ahead)
    bits = [1 << b for b in range(wide.bit_length() - 1)]
    stages = [(bits[0],), tuple(bits[1:3]), *[(bit,) for bit in bits[3:]]]
    high = bits[-1]
    cross, stay = pl.pallas_call(
        merge_kernel,
        out_shape=(
            jax.ShapeDtypeStruct((part, width), bf16),
            jax.ShapeDtypeStruct((part, width + model), bf16),
        ),
        in_specs=[VMEM] * 3,
        out_specs=(VMEM,) * 2,
        compiler_params=pltpu.CompilerParams(vmem_limit_bytes=2 * MIB),
        name="merge",
    )(mixed, behind, residual)
    far_cross = lax.ppermute(
        cross,
        ("wide", "head"),
        [(i * heads + h, (i ^ high) * heads + 1 - h) for i in range(wide) for h in range(heads)],
    )
    far_stay = swapped(stay, high)
    near_cross = lax.ppermute(cross, "head", [(h, 1 - h) for h in range(heads)])
    middle, gathered = pl.pallas_call(
        norm_kernel,
        out_shape=(
            jax.ShapeDtypeStruct((part, model), f32),
            jax.ShapeDtypeStruct((2 * part, model), bf16),
        ),
        in_specs=[VMEM] * 5,
        out_specs=(VMEM,) * 2,
        compiler_params=pltpu.CompilerParams(vmem_limit_bytes=2 * MIB),
        cost_estimate=WHILE_EXCHANGING,
        name="norm",
    )(stay, near_cross, far_stay, far_cross, gain)
    for stage in stages[-2:0:-1]:
        gathered = joined([gathered] + [swapped(gathered, s) for s in combined(stage)])
    far = swapped(gathered, bits[0])

    half = gathered.shape[0]
    kept, sent = pl.pallas_call(
        feed_kernel,
        out_shape=(
            jax.ShapeDtypeStruct((half, model), f32),
            jax.ShapeDtypeStruct((half, model), bf16),
        ),
        in_specs=[SMEM] * 5 + [VMEM] * 5,
        out_specs=(VMEM,) * 2,
        scratch_shapes=[
            pltpu.VMEM((columns, 2 * half, BLK), bf16),
            pltpu.VMEM((2 * half, model), f32),
        ],
        compiler_params=pltpu.CompilerParams(
            vmem_limit_bytes=2 * half * model * 4 + half * model * 6 + 4 * MIB
        ),
        name="feed",
    )(*lists, gathered, far, gate_blocks, up_blocks, down_blocks)

    total = kept + swapped(sent, bits[0]).astype(f32)
    for stage in stages[1:]:
        half = half >> len(stage)
        kept, sent = total[:half], total[half:].astype(bf16)
        total = kept
        for i, s in enumerate(combined(stage)):
            total = total + swapped(sent[i * half : (i + 1) * half], s).astype(f32)
    return (middle + total).astype(bf16)


def solution(mesh):
    placed = (
        P("wide", "head"),
        P("wide", "head"),
        P("wide", "head"),
        P(None, "wide", None, "head"),
        P("wide", None),
        P("wide"),
        P("wide"),
        P(("wide", "head"), None),
        P(),
        P("wide", None, None, None),
        P("wide", None, None, None),
        P("wide", None),
        P("wide", None),
        P("wide", None),
        P("wide", None, None, None),
        P("wide", None),
        P("wide", None),
    )
    return jax.shard_map(
        per_device, mesh=mesh, in_specs=placed, out_specs=P(("wide", "head"), None), check_vma=False
    )
```

```python
import functools
import math

import jax
import jax.numpy as jnp
from jax import lax
from jax.experimental import pallas as pl
from jax.experimental.pallas import tpu as pltpu
from jax.sharding import PartitionSpec as P

HD = 128
BLK = 128
PACKED = 16
GROUP = 4
DEAD = -1e30
MIB = 1024 * 1024
WHILE_EXCHANGING = pl.CostEstimate(flops=20 * 10**9, bytes_accessed=64 * MIB, transcendentals=0)

VMEM = pl.BlockSpec(memory_space=pltpu.VMEM)
SMEM = pl.BlockSpec(memory_space=pltpu.SMEM)
HBM = pl.BlockSpec(memory_space=pltpu.HBM)


def in_hbm(arrays):
    return [pltpu.with_memory_space_constraint(a, pltpu.HBM) for a in arrays]


def like(array):
    return jax.ShapeDtypeStruct(array.shape, array.dtype)


def copies(pairs, sems):
    return [
        pltpu.make_async_copy(source, target, sems.at[i])
        for i, (source, target) in enumerate(pairs)
    ]


def pack_kernel(query_hbm, key_hbm, value_hbm, parent_hbm, packed_ref, parent_ref, sems):
    rows, width = query_hbm.shape
    kv_width = key_hbm.shape[1]
    moves = copies(
        (
            (parent_hbm, parent_ref),
            (query_hbm, packed_ref.at[:, pl.ds(0, width)]),
            (key_hbm, packed_ref.at[:, pl.ds(width, kv_width)]),
            (value_hbm, packed_ref.at[:, pl.ds(width + kv_width, kv_width)]),
        ),
        sems,
    )
    for move in moves:
        move.start()
    moves[0].wait()
    first = lax.axis_index("wide") * rows
    row = lax.broadcasted_iota(jnp.int32, (rows, HD), 0)
    parent = jnp.zeros((rows, HD), jnp.int32)
    for r in range(rows):
        parent = jnp.where(row == r, parent_ref[r] - first, parent)
    packed_ref[:, width + 2 * kv_width :] = parent.astype(jnp.float32).astype(jnp.bfloat16)
    for move in moves[1:]:
        move.wait()


def attend_kernel(groups, per_group, shift, packed_ref, pool_ref, owner_ref, *refs):
    out_ref = refs[-1]
    rows = packed_ref.shape[0]
    kv_width = groups * HD
    width = kv_width * per_group
    spots = owner_ref.shape[0]
    f32, bf16 = jnp.float32, jnp.bfloat16

    query = packed_ref[:, :width].astype(f32)
    tall = []
    for g in range(groups):
        heads = range(g * per_group, (g + 1) * per_group)
        block = jnp.concatenate([query[:, j * HD : (j + 1) * HD] for j in heads], axis=0)
        gap = jnp.zeros_like(block)
        tall.append(jnp.concatenate([block if i == g else gap for i in range(groups)], axis=1))
    tall = jnp.concatenate(tall, axis=0).astype(bf16)
    lanes = tall.shape[0]

    branch = lax.broadcasted_iota(jnp.int32, (1, lanes), 1) % rows
    code = packed_ref[:, width + 2 * kv_width :].astype(f32) + shift
    parent = jnp.zeros((1, lanes), f32)
    for r in range(rows):
        parent = jnp.where(branch == r, code[r : r + 1, :], parent)
    gap = jnp.zeros((PACKED - rows, kv_width), f32)
    key_own, value_own = (
        jnp.concatenate([packed_ref[:, start : start + kv_width].astype(f32), gap], axis=0).astype(bf16)
        for start in (width, width + kv_width)
    )
    of_branch = lax.broadcasted_iota(jnp.int32, (PACKED, lanes), 0) == branch

    def against(keys):
        return lax.dot_general(keys, tall, (((1,), (1,)), ((), ())), preferred_element_type=f32)

    def mixed(weights, values):
        return lax.dot_general(
            weights, values, (((0,), (0,)), ((), ())), preferred_element_type=f32
        )

    factor = 1.0 / math.sqrt(HD)
    scores = against(pool_ref[0].reshape(spots, kv_width)) * factor
    scores = jnp.where(owner_ref[...] == parent, scores, DEAD)
    own = jnp.sum(jnp.where(of_branch, against(key_own), 0.0), axis=0, keepdims=True) * factor
    top = jnp.maximum(jnp.max(scores, axis=0, keepdims=True), own)
    expo = jnp.exp(scores - top)
    own_expo = jnp.exp(own - top)
    share = 1.0 / (jnp.sum(expo, axis=0, keepdims=True) + own_expo)
    mixture = mixed((expo * share).astype(bf16), pool_ref[1].reshape(spots, kv_width))
    own_weight = jnp.where(of_branch, own_expo * share, 0.0).astype(bf16)
    mixture = mixture + mixed(own_weight, value_own)
    here = (code[:, :1] >= 0) & (code[:, :1] < rows)
    for j in range(groups * per_group):
        g = j // per_group
        out_ref[:, j * HD : (j + 1) * HD] = jnp.where(
            here, mixture[j * rows : (j + 1) * rows, g * HD : (g + 1) * HD], 0.0
        ).astype(bf16)


def prepare_kernel(count, *refs):
    page_hbm, length_hbm, sources = refs[0], refs[1], refs[2 : 2 + count]
    lists, refs = refs[2 + count : 7 + count], refs[7 + count :]
    owner_ref, targets, keeps_ref, scales_ref = refs[0], refs[1 : 1 + count], *refs[1 + count : 3 + count]
    page_ref, length_ref, sems = refs[3 + count :]
    stacked = [keeps_ref.at[i] for i in range(2)] + [scales_ref.at[i] for i in range(3)]
    moves = copies(
        (
            (page_hbm, page_ref),
            (length_hbm, length_ref),
            *zip(sources, targets),
            *zip(lists, stacked),
        ),
        sems,
    )
    for move in moves:
        move.start()
    moves[0].wait()
    moves[1].wait()
    page = sources[0].shape[2]
    offset = lax.broadcasted_iota(jnp.int32, (page, HD), 0)
    for r in range(page_ref.shape[0]):
        for i in range(page_ref.shape[1]):
            places = pl.ds(pl.multiple_of(page_ref[r, i] * page, page), page)
            owner_ref[places, :] = jnp.where(offset < length_ref[r] - i * page, float(r), -1.0)
    for move in moves[2:]:
        move.wait()


def merge_kernel(own_ref, behind_ref, residual_ref, cross_ref, stay_ref):
    head = lax.axis_index("head")
    part, width = cross_ref.shape
    both = own_ref[...].astype(jnp.float32) + behind_ref[...].astype(jnp.float32)
    low, high = both[:part], both[part : 2 * part]
    cross_ref[...] = jnp.where(head == 0, high, low).astype(jnp.bfloat16)
    stay_ref[:, :width] = jnp.where(head == 0, low, high).astype(jnp.bfloat16)
    stay_ref[:, width:] = residual_ref[...]


def norm_kernel(stay_ref, cross_ref, far_stay_ref, far_cross_ref, gain_ref, middle_ref, normed_ref):
    head = lax.axis_index("head")
    part, half = cross_ref.shape
    f32 = jnp.float32
    for i, (stay, cross) in enumerate(((stay_ref, cross_ref), (far_stay_ref, far_cross_ref))):
        same, other = stay[:, :half].astype(f32), cross[...].astype(f32)
        low = stay[:, half : 2 * half].astype(f32) + jnp.where(head == 0, same, other)
        high = stay[:, 2 * half :].astype(f32) + jnp.where(head == 0, other, same)
        if i == 0:
            middle_ref[:, :half] = low
            middle_ref[:, half:] = high
        square = jnp.sum(low * low, axis=-1, keepdims=True)
        square = square + jnp.sum(high * high, axis=-1, keepdims=True)
        scale = lax.rsqrt(square / (2 * half) + 1e-05)
        rows = slice(i * part, (i + 1) * part)
        normed_ref[rows, :half] = (low * scale * gain_ref[:, :half]).astype(jnp.bfloat16)
        normed_ref[rows, half:] = (high * scale * gain_ref[:, half:]).astype(jnp.bfloat16)


def feed_kernel(
    keeps_ref, scales_ref, near_ref, far_ref, gate_ref, up_ref, down_ref,
    stay_ref, send_ref, far_total,
):
    _, columns, keep = keeps_ref.shape
    half = near_ref.shape[0]
    stay_ref[...] = jnp.zeros_like(stay_ref)
    far_total[...] = jnp.zeros_like(far_total)

    def block(which, c, k):
        return pl.ds(pl.multiple_of(keeps_ref[which, c, k] * BLK, BLK), BLK)

    hidden = []
    for c in range(columns):
        gate_sum = jnp.zeros((2 * half, BLK), jnp.float32)
        up_sum = jnp.zeros((2 * half, BLK), jnp.float32)
        for k in range(keep):
            where = block(0, c, k)
            picked = jnp.concatenate([near_ref[:, where], far_ref[:, where]], axis=0)
            both = jnp.dot(
                picked, jnp.concatenate([gate_ref[c, k], up_ref[c, k]], axis=1),
                preferred_element_type=jnp.float32,
            )
            gate_sum += scales_ref[0, c, k] * both[:, :BLK]
            up_sum += scales_ref[1, c, k] * both[:, BLK:]
        hidden.append((gate_sum / (1.0 + jnp.exp(-gate_sum)) * up_sum).astype(jnp.bfloat16))
    for c in range(columns):
        for start in range(0, keep, GROUP):
            group = range(start, start + GROUP)
            places = [block(1, c, k) for k in group]
            near_sums = [stay_ref[:, where] for where in places]
            far_sums = [far_total[:, where] for where in places]
            for i in range(0, GROUP, 2):
                both = jnp.dot(
                    hidden[c],
                    jnp.concatenate([down_ref[c, group[i]], down_ref[c, group[i + 1]]], axis=1),
                    preferred_element_type=jnp.float32,
                )
                for j in range(2):
                    term = scales_ref[2, c, group[i + j]] * both[:, j * BLK : (j + 1) * BLK]
                    near_sums[i + j] += term[:half]
                    far_sums[i + j] += term[half:]
            for where, near_sum, far_sum in zip(places, near_sums, far_sums):
                stay_ref[:, where] = near_sum
                far_total[:, where] = far_sum
    send_ref[...] = far_total[...].astype(jnp.bfloat16)


def join_kernel(*refs):
    out_ref = refs[-1]
    height = refs[0].shape[0]
    for i, ref in enumerate(refs[:-1]):
        out_ref[i * height : (i + 1) * height, :] = ref[...]


def joined(blocks):
    height, width = blocks[0].shape
    return pl.pallas_call(
        join_kernel,
        out_shape=jax.ShapeDtypeStruct((len(blocks) * height, width), blocks[0].dtype),
        in_specs=[VMEM] * len(blocks),
        out_specs=VMEM,
        compiler_params=pltpu.CompilerParams(vmem_limit_bytes=2 * MIB),
        cost_estimate=WHILE_EXCHANGING,
        name="join",
    )(*blocks)


def swapped(block, bits):
    return lax.ppermute(block, "wide", [(i, i ^ bits) for i in range(lax.axis_size("wide"))])


def combined(bits):
    sums = [0]
    for bit in bits:
        sums += [s + bit for s in sums]
    return sums[1:]


def per_device(
    branch_query, key_new, value_new, pool_pages, page_table, tail_length, parent_row, residual,
    norm_gain, gate_blocks, up_blocks, gate_up_keep, gate_scale, up_scale, down_blocks, down_keep,
    down_scale,
):
    bf16, f32 = jnp.bfloat16, jnp.float32
    wide, heads = lax.axis_size("wide"), lax.axis_size("head")
    rows, width = branch_query.shape
    kv_width = key_new.shape[1]
    groups = kv_width // HD
    per_group = width // kv_width
    part, model = residual.shape
    columns = gate_blocks.shape[0]

    own = pl.pallas_call(
        pack_kernel,
        out_shape=jax.ShapeDtypeStruct((rows, width + 2 * kv_width + HD), bf16),
        in_specs=[HBM] * 4,
        out_specs=VMEM,
        scratch_shapes=[
            pltpu.SMEM(parent_row.shape, jnp.int32),
            pltpu.SemaphoreType.DMA((4,)),
        ],
        compiler_params=pltpu.CompilerParams(vmem_limit_bytes=2 * MIB),
        name="pack",
    )(*in_hbm([branch_query, key_new, value_new, parent_row]))
    following = lax.ppermute(own, "wide", [(i, i - 1) for i in range(1, wide)])

    stored = [pool_pages, residual, norm_gain.reshape(1, model)]
    lists = [gate_up_keep, down_keep, gate_scale, up_scale, down_scale]
    spots = pool_pages.shape[1] * pool_pages.shape[2]
    owner, pool, residual, gain, keeps, scales = pl.pallas_call(
        functools.partial(prepare_kernel, len(stored)),
        out_shape=(
            jax.ShapeDtypeStruct((spots, HD), f32),
            *[like(a) for a in stored],
            jax.ShapeDtypeStruct((2, *gate_up_keep.shape), jnp.int32),
            jax.ShapeDtypeStruct((3, *gate_scale.shape), f32),
        ),
        in_specs=[HBM] * (2 + len(stored) + len(lists)),
        out_specs=(VMEM,) * (3 + len(stored)),
        scratch_shapes=[
            pltpu.SMEM(page_table.shape, jnp.int32),
            pltpu.SMEM(tail_length.shape, jnp.int32),
            pltpu.SemaphoreType.DMA((2 + len(stored) + len(lists),)),
        ],
        compiler_params=pltpu.CompilerParams(vmem_limit_bytes=2 * MIB),
        cost_estimate=pl.CostEstimate(flops=0, bytes_accessed=8 * MIB, transcendentals=0),
        name="prepare",
    )(*in_hbm([page_table, tail_length, *stored, *lists]))

    def attended(packed, shift, *after):
        return pl.pallas_call(
            functools.partial(attend_kernel, groups, per_group, shift),
            out_shape=jax.ShapeDtypeStruct((rows, width), bf16),
            in_specs=[VMEM] * (3 + len(after)),
            out_specs=VMEM,
            compiler_params=pltpu.CompilerParams(vmem_limit_bytes=6 * MIB),
            name="attend",
        )(packed, pool, owner, *after)

    ahead = attended(following, rows)
    behind = lax.ppermute(ahead, "wide", [(i, i + 1) for i in range(wide - 1)])
    mixed = attended(own, 0, ahead)
    bits = [1 << b for b in range(wide.bit_length() - 1)]
    stages = [(bits[0],), tuple(bits[1:3]), *[(bit,) for bit in bits[3:]]]
    high = bits[-1]
    cross, stay = pl.pallas_call(
        merge_kernel,
        out_shape=(
            jax.ShapeDtypeStruct((part, width), bf16),
            jax.ShapeDtypeStruct((part, width + model), bf16),
        ),
        in_specs=[VMEM] * 3,
        out_specs=(VMEM,) * 2,
        compiler_params=pltpu.CompilerParams(vmem_limit_bytes=2 * MIB),
        name="merge",
    )(mixed, behind, residual)
    far_cross = lax.ppermute(
        cross,
        ("wide", "head"),
        [(i * heads + h, (i ^ high) * heads + 1 - h) for i in range(wide) for h in range(heads)],
    )
    far_stay = swapped(stay, high)
    near_cross = lax.ppermute(cross, "head", [(h, 1 - h) for h in range(heads)])
    middle, gathered = pl.pallas_call(
        norm_kernel,
        out_shape=(
            jax.ShapeDtypeStruct((part, model), f32),
            jax.ShapeDtypeStruct((2 * part, model), bf16),
        ),
        in_specs=[VMEM] * 5,
        out_specs=(VMEM,) * 2,
        compiler_params=pltpu.CompilerParams(vmem_limit_bytes=2 * MIB),
        cost_estimate=WHILE_EXCHANGING,
        name="norm",
    )(stay, near_cross, far_stay, far_cross, gain)
    for stage in stages[-2:0:-1]:
        gathered = joined([gathered] + [swapped(gathered, s) for s in combined(stage)])
    far = swapped(gathered, bits[0])

    half = gathered.shape[0]
    kept, sent = pl.pallas_call(
        feed_kernel,
        out_shape=(
            jax.ShapeDtypeStruct((half, model), f32),
            jax.ShapeDtypeStruct((half, model), bf16),
        ),
        in_specs=[SMEM] * 2 + [VMEM] * 5,
        out_specs=(VMEM,) * 2,
        scratch_shapes=[pltpu.VMEM((half, model), f32)],
        compiler_params=pltpu.CompilerParams(vmem_limit_bytes=half * model * 10 + 6 * MIB),
        name="feed",
    )(keeps, scales, gathered, far, gate_blocks, up_blocks, down_blocks)

    total = kept + swapped(sent, bits[0]).astype(f32)
    for stage in stages[1:]:
        half = half >> len(stage)
        kept, sent = total[:half], total[half:].astype(bf16)
        total = kept
        for i, s in enumerate(combined(stage)):
            total = total + swapped(sent[i * half : (i + 1) * half], s).astype(f32)
    return (middle + total).astype(bf16)


def solution(mesh):
    placed = (
        P("wide", "head"),
        P("wide", "head"),
        P("wide", "head"),
        P(None, "wide", None, "head"),
        P("wide", None),
        P("wide"),
        P("wide"),
        P(("wide", "head"), None),
        P(),
        P("wide", None, None, None),
        P("wide", None, None, None),
        P("wide", None),
        P("wide", None),
        P("wide", None),
        P("wide", None, None, None),
        P("wide", None),
        P("wide", None),
    )
    return jax.shard_map(
        per_device, mesh=mesh, in_specs=placed, out_specs=P(("wide", "head"), None), check_vma=False
    )
```

```python
import functools
import math

import jax
import jax.numpy as jnp
from jax import lax
from jax.experimental import pallas as pl
from jax.experimental.pallas import tpu as pltpu
from jax.sharding import PartitionSpec as P

HD = 128
BLK = 128
PACKED = 16
GROUP = 4
DEAD = -1e30
MIB = 1024 * 1024
WHILE_EXCHANGING = pl.CostEstimate(flops=20 * 10**9, bytes_accessed=64 * MIB, transcendentals=0)

VMEM = pl.BlockSpec(memory_space=pltpu.VMEM)
SMEM = pl.BlockSpec(memory_space=pltpu.SMEM)
HBM = pl.BlockSpec(memory_space=pltpu.HBM)


def in_hbm(arrays):
    return [pltpu.with_memory_space_constraint(a, pltpu.HBM) for a in arrays]


def like(array):
    return jax.ShapeDtypeStruct(array.shape, array.dtype)


def copies(pairs, sems):
    return [
        pltpu.make_async_copy(source, target, sems.at[i])
        for i, (source, target) in enumerate(pairs)
    ]


def pack_kernel(query_hbm, key_hbm, value_hbm, parent_hbm, packed_ref, parent_ref, sems):
    rows, width = query_hbm.shape
    kv_width = key_hbm.shape[1]
    moves = copies(
        (
            (parent_hbm, parent_ref),
            (query_hbm, packed_ref.at[:, pl.ds(0, width)]),
            (key_hbm, packed_ref.at[:, pl.ds(width, kv_width)]),
            (value_hbm, packed_ref.at[:, pl.ds(width + kv_width, kv_width)]),
        ),
        sems,
    )
    for move in moves:
        move.start()
    moves[0].wait()
    first = lax.axis_index("wide") * rows
    row = lax.broadcasted_iota(jnp.int32, (rows, HD), 0)
    parent = jnp.zeros((rows, HD), jnp.int32)
    for r in range(rows):
        parent = jnp.where(row == r, parent_ref[r] - first, parent)
    packed_ref[:, width + 2 * kv_width :] = parent.astype(jnp.float32).astype(jnp.bfloat16)
    for move in moves[1:]:
        move.wait()


def attend_kernel(groups, per_group, shift, packed_ref, pool_ref, owner_ref, *refs):
    out_ref = refs[-1]
    rows = packed_ref.shape[0]
    kv_width = groups * HD
    width = kv_width * per_group
    spots = owner_ref.shape[0]
    f32, bf16 = jnp.float32, jnp.bfloat16

    query = packed_ref[:, :width].astype(f32)
    tall = []
    for g in range(groups):
        heads = range(g * per_group, (g + 1) * per_group)
        block = jnp.concatenate([query[:, j * HD : (j + 1) * HD] for j in heads], axis=0)
        gap = jnp.zeros_like(block)
        tall.append(jnp.concatenate([block if i == g else gap for i in range(groups)], axis=1))
    tall = jnp.concatenate(tall, axis=0).astype(bf16)
    lanes = tall.shape[0]

    branch = lax.broadcasted_iota(jnp.int32, (1, lanes), 1) % rows
    code = packed_ref[:, width + 2 * kv_width :].astype(f32) + shift
    parent = jnp.zeros((1, lanes), f32)
    for r in range(rows):
        parent = jnp.where(branch == r, code[r : r + 1, :], parent)
    gap = jnp.zeros((PACKED - rows, kv_width), f32)
    key_own, value_own = (
        jnp.concatenate([packed_ref[:, start : start + kv_width].astype(f32), gap], axis=0).astype(bf16)
        for start in (width, width + kv_width)
    )
    of_branch = lax.broadcasted_iota(jnp.int32, (PACKED, lanes), 0) == branch

    def against(keys):
        return lax.dot_general(keys, tall, (((1,), (1,)), ((), ())), preferred_element_type=f32)

    def mixed(weights, values):
        return lax.dot_general(
            weights, values, (((0,), (0,)), ((), ())), preferred_element_type=f32
        )

    factor = 1.0 / math.sqrt(HD)
    scores = against(pool_ref[0].reshape(spots, kv_width)) * factor
    scores = jnp.where(owner_ref[...] == parent, scores, DEAD)
    own = jnp.sum(jnp.where(of_branch, against(key_own), 0.0), axis=0, keepdims=True) * factor
    top = jnp.maximum(jnp.max(scores, axis=0, keepdims=True), own)
    expo = jnp.exp(scores - top)
    own_expo = jnp.exp(own - top)
    share = 1.0 / (jnp.sum(expo, axis=0, keepdims=True) + own_expo)
    mixture = mixed((expo * share).astype(bf16), pool_ref[1].reshape(spots, kv_width))
    own_weight = jnp.where(of_branch, own_expo * share, 0.0).astype(bf16)
    mixture = mixture + mixed(own_weight, value_own)
    here = (code[:, :1] >= 0) & (code[:, :1] < rows)
    for j in range(groups * per_group):
        g = j // per_group
        out_ref[:, j * HD : (j + 1) * HD] = jnp.where(
            here, mixture[j * rows : (j + 1) * rows, g * HD : (g + 1) * HD], 0.0
        ).astype(bf16)


def prepare_kernel(count, *refs):
    page_hbm, length_hbm, sources = refs[0], refs[1], refs[2 : 2 + count]
    lists, refs = refs[2 + count : 7 + count], refs[7 + count :]
    owner_ref, targets, keeps_ref, scales_ref = refs[0], refs[1 : 1 + count], *refs[1 + count : 3 + count]
    page_ref, length_ref, sems = refs[3 + count :]
    stacked = [keeps_ref.at[i] for i in range(2)] + [scales_ref.at[i] for i in range(3)]
    moves = copies(
        (
            (page_hbm, page_ref),
            (length_hbm, length_ref),
            *zip(sources, targets),
            *zip(lists, stacked),
        ),
        sems,
    )
    for move in moves:
        move.start()
    moves[0].wait()
    moves[1].wait()
    page = sources[0].shape[2]
    offset = lax.broadcasted_iota(jnp.int32, (page, HD), 0)
    for r in range(page_ref.shape[0]):
        for i in range(page_ref.shape[1]):
            places = pl.ds(pl.multiple_of(page_ref[r, i] * page, page), page)
            owner_ref[places, :] = jnp.where(offset < length_ref[r] - i * page, float(r), -1.0)
    for move in moves[2:]:
        move.wait()


def merge_kernel(own_ref, behind_ref, residual_ref, cross_ref, stay_ref):
    head = lax.axis_index("head")
    part, width = cross_ref.shape
    both = own_ref[...].astype(jnp.float32) + behind_ref[...].astype(jnp.float32)
    low, high = both[:part], both[part : 2 * part]
    cross_ref[...] = jnp.where(head == 0, high, low).astype(jnp.bfloat16)
    stay_ref[:, :width] = jnp.where(head == 0, low, high).astype(jnp.bfloat16)
    stay_ref[:, width:] = residual_ref[...]


def norm_kernel(stay_ref, cross_ref, far_stay_ref, far_cross_ref, gain_ref, middle_ref, normed_ref):
    head = lax.axis_index("head")
    part, half = cross_ref.shape
    f32 = jnp.float32
    for i, (stay, cross) in enumerate(((stay_ref, cross_ref), (far_stay_ref, far_cross_ref))):
        same, other = stay[:, :half].astype(f32), cross[...].astype(f32)
        low = stay[:, half : 2 * half].astype(f32) + jnp.where(head == 0, same, other)
        high = stay[:, 2 * half :].astype(f32) + jnp.where(head == 0, other, same)
        if i == 0:
            middle_ref[:, :half] = low
            middle_ref[:, half:] = high
        square = jnp.sum(low * low, axis=-1, keepdims=True)
        square = square + jnp.sum(high * high, axis=-1, keepdims=True)
        scale = lax.rsqrt(square / (2 * half) + 1e-05)
        rows = slice(i * part, (i + 1) * part)
        normed_ref[rows, :half] = (low * scale * gain_ref[:, :half]).astype(jnp.bfloat16)
        normed_ref[rows, half:] = (high * scale * gain_ref[:, half:]).astype(jnp.bfloat16)


def feed_kernel(
    keeps_ref, scales_ref, near_ref, far_ref, gate_ref, up_ref, down_ref,
    stay_ref, send_ref, far_total,
):
    _, columns, keep = keeps_ref.shape
    half = near_ref.shape[0]
    stay_ref[...] = jnp.zeros_like(stay_ref)
    far_total[...] = jnp.zeros_like(far_total)

    def block(which, c, k):
        return pl.ds(pl.multiple_of(keeps_ref[which, c, k] * BLK, BLK), BLK)

    hidden = []
    for c in range(columns):
        gate_sum = jnp.zeros((2 * half, BLK), jnp.float32)
        up_sum = jnp.zeros((2 * half, BLK), jnp.float32)
        for k in range(keep):
            where = block(0, c, k)
            picked = jnp.concatenate([near_ref[:, where], far_ref[:, where]], axis=0)
            both = jnp.dot(
                picked, jnp.concatenate([gate_ref[c, k], up_ref[c, k]], axis=1),
                preferred_element_type=jnp.float32,
            )
            gate_sum += scales_ref[0, c, k] * both[:, :BLK]
            up_sum += scales_ref[1, c, k] * both[:, BLK:]
        hidden.append((gate_sum / (1.0 + jnp.exp(-gate_sum)) * up_sum).astype(jnp.bfloat16))
    for c in range(columns):
        for start in range(0, keep, GROUP):
            group = range(start, start + GROUP)
            places = [block(1, c, k) for k in group]
            near_sums = [stay_ref[:, where] for where in places]
            far_sums = [far_total[:, where] for where in places]
            for i in range(0, GROUP, 2):
                both = jnp.dot(
                    hidden[c],
                    jnp.concatenate([down_ref[c, group[i]], down_ref[c, group[i + 1]]], axis=1),
                    preferred_element_type=jnp.float32,
                )
                for j in range(2):
                    term = scales_ref[2, c, group[i + j]] * both[:, j * BLK : (j + 1) * BLK]
                    near_sums[i + j] += term[:half]
                    far_sums[i + j] += term[half:]
            for where, near_sum, far_sum in zip(places, near_sums, far_sums):
                stay_ref[:, where] = near_sum
                far_total[:, where] = far_sum
    send_ref[...] = far_total[...].astype(jnp.bfloat16)


def join_kernel(*refs):
    out_ref = refs[-1]
    height = refs[0].shape[0]
    for i, ref in enumerate(refs[:-1]):
        out_ref[i * height : (i + 1) * height, :] = ref[...]


def joined(blocks):
    height, width = blocks[0].shape
    return pl.pallas_call(
        join_kernel,
        out_shape=jax.ShapeDtypeStruct((len(blocks) * height, width), blocks[0].dtype),
        in_specs=[VMEM] * len(blocks),
        out_specs=VMEM,
        compiler_params=pltpu.CompilerParams(vmem_limit_bytes=2 * MIB),
        name="join",
    )(*blocks)


def sum_kernel(count, kept_ref, *refs):
    blocks, kept_out, sent = refs[:count], refs[count], refs[count + 1 :]
    height = kept_out.shape[0]
    for i, out_ref in enumerate((kept_out, *sent)):
        rows = slice(i * height, (i + 1) * height)
        total = kept_ref[rows, :]
        for block in blocks:
            total = total + block[rows, :].astype(jnp.float32)
        out_ref[...] = total.astype(out_ref.dtype)


def summed(kept, blocks, parts):
    height, width = kept.shape
    part = (height // parts, width)
    return pl.pallas_call(
        functools.partial(sum_kernel, len(blocks)),
        out_shape=(
            jax.ShapeDtypeStruct(part, jnp.float32),
            *[jax.ShapeDtypeStruct(part, jnp.bfloat16)] * (parts - 1),
        ),
        in_specs=[VMEM] * (1 + len(blocks)),
        out_specs=(VMEM,) * parts,
        compiler_params=pltpu.CompilerParams(vmem_limit_bytes=2 * MIB),
        name="sum",
    )(kept, *blocks)


def swapped(block, bits):
    return lax.ppermute(block, "wide", [(i, i ^ bits) for i in range(lax.axis_size("wide"))])


def combined(bits):
    sums = [0]
    for bit in bits:
        sums += [s + bit for s in sums]
    return sums[1:]


def per_device(
    branch_query, key_new, value_new, pool_pages, page_table, tail_length, parent_row, residual,
    norm_gain, gate_blocks, up_blocks, gate_up_keep, gate_scale, up_scale, down_blocks, down_keep,
    down_scale,
):
    bf16, f32 = jnp.bfloat16, jnp.float32
    wide, heads = lax.axis_size("wide"), lax.axis_size("head")
    rows, width = branch_query.shape
    kv_width = key_new.shape[1]
    groups = kv_width // HD
    per_group = width // kv_width
    part, model = residual.shape
    columns = gate_blocks.shape[0]

    own = pl.pallas_call(
        pack_kernel,
        out_shape=jax.ShapeDtypeStruct((rows, width + 2 * kv_width + HD), bf16),
        in_specs=[HBM] * 4,
        out_specs=VMEM,
        scratch_shapes=[
            pltpu.SMEM(parent_row.shape, jnp.int32),
            pltpu.SemaphoreType.DMA((4,)),
        ],
        compiler_params=pltpu.CompilerParams(vmem_limit_bytes=2 * MIB),
        name="pack",
    )(*in_hbm([branch_query, key_new, value_new, parent_row]))
    following = lax.ppermute(own, "wide", [(i, i - 1) for i in range(1, wide)])

    stored = [pool_pages, residual, norm_gain.reshape(1, model)]
    lists = [gate_up_keep, down_keep, gate_scale, up_scale, down_scale]
    spots = pool_pages.shape[1] * pool_pages.shape[2]
    owner, pool, residual, gain, keeps, scales = pl.pallas_call(
        functools.partial(prepare_kernel, len(stored)),
        out_shape=(
            jax.ShapeDtypeStruct((spots, HD), f32),
            *[like(a) for a in stored],
            jax.ShapeDtypeStruct((2, *gate_up_keep.shape), jnp.int32),
            jax.ShapeDtypeStruct((3, *gate_scale.shape), f32),
        ),
        in_specs=[HBM] * (2 + len(stored) + len(lists)),
        out_specs=(VMEM,) * (3 + len(stored)),
        scratch_shapes=[
            pltpu.SMEM(page_table.shape, jnp.int32),
            pltpu.SMEM(tail_length.shape, jnp.int32),
            pltpu.SemaphoreType.DMA((2 + len(stored) + len(lists),)),
        ],
        compiler_params=pltpu.CompilerParams(vmem_limit_bytes=2 * MIB),
        cost_estimate=pl.CostEstimate(flops=0, bytes_accessed=8 * MIB, transcendentals=0),
        name="prepare",
    )(*in_hbm([page_table, tail_length, *stored, *lists]))

    def attended(packed, shift, *after):
        return pl.pallas_call(
            functools.partial(attend_kernel, groups, per_group, shift),
            out_shape=jax.ShapeDtypeStruct((rows, width), bf16),
            in_specs=[VMEM] * (3 + len(after)),
            out_specs=VMEM,
            compiler_params=pltpu.CompilerParams(vmem_limit_bytes=6 * MIB),
            name="attend",
        )(packed, pool, owner, *after)

    ahead = attended(following, rows)
    behind = lax.ppermute(ahead, "wide", [(i, i + 1) for i in range(wide - 1)])
    mixed = attended(own, 0, ahead)
    bits = [1 << b for b in range(wide.bit_length() - 1)]
    stages = [(bits[0],), tuple(bits[1:3]), *[(bit,) for bit in bits[3:]]]
    sum_stages = stages[1:]
    high = bits[-1]
    cross, stay = pl.pallas_call(
        merge_kernel,
        out_shape=(
            jax.ShapeDtypeStruct((part, width), bf16),
            jax.ShapeDtypeStruct((part, width + model), bf16),
        ),
        in_specs=[VMEM] * 3,
        out_specs=(VMEM,) * 2,
        compiler_params=pltpu.CompilerParams(vmem_limit_bytes=2 * MIB),
        cost_estimate=WHILE_EXCHANGING,
        name="merge",
    )(mixed, behind, residual)
    far_cross = lax.ppermute(
        cross,
        ("wide", "head"),
        [(i * heads + h, (i ^ high) * heads + 1 - h) for i in range(wide) for h in range(heads)],
    )
    far_stay = swapped(stay, high)
    near_cross = lax.ppermute(cross, "head", [(h, 1 - h) for h in range(heads)])
    middle, gathered = pl.pallas_call(
        norm_kernel,
        out_shape=(
            jax.ShapeDtypeStruct((part, model), f32),
            jax.ShapeDtypeStruct((2 * part, model), bf16),
        ),
        in_specs=[VMEM] * 5,
        out_specs=(VMEM,) * 2,
        compiler_params=pltpu.CompilerParams(vmem_limit_bytes=2 * MIB),
        name="norm",
    )(stay, near_cross, far_stay, far_cross, gain)
    for stage in stages[-2:0:-1]:
        gathered = joined([gathered] + [swapped(gathered, s) for s in combined(stage)])
    far = swapped(gathered, bits[0])

    half = gathered.shape[0]
    kept, sent = pl.pallas_call(
        feed_kernel,
        out_shape=(
            jax.ShapeDtypeStruct((half, model), f32),
            jax.ShapeDtypeStruct((half, model), bf16),
        ),
        in_specs=[SMEM] * 2 + [VMEM] * 5,
        out_specs=(VMEM,) * 2,
        scratch_shapes=[pltpu.VMEM((half, model), f32)],
        compiler_params=pltpu.CompilerParams(vmem_limit_bytes=half * model * 10 + 6 * MIB),
        name="feed",
    )(keeps, scales, gathered, far, gate_blocks, up_blocks, down_blocks)

    blocks = [swapped(sent, bits[0])]
    for stage in sum_stages:
        sums = combined(stage)
        kept, *sent = summed(kept, blocks, 1 + len(sums))
        blocks = [swapped(block, s) for block, s in sorted(zip(sent, sums), key=lambda p: -bin(p[1]).count('1'))]
    total = middle + kept
    for block in blocks:
        total = total + block.astype(f32)
    return total.astype(bf16)


def solution(mesh):
    placed = (
        P("wide", "head"),
        P("wide", "head"),
        P("wide", "head"),
        P(None, "wide", None, "head"),
        P("wide", None),
        P("wide"),
        P("wide"),
        P(("wide", "head"), None),
        P(),
        P("wide", None, None, None),
        P("wide", None, None, None),
        P("wide", None),
        P("wide", None),
        P("wide", None),
        P("wide", None, None, None),
        P("wide", None),
        P("wide", None),
    )
    return jax.shard_map(
        per_device, mesh=mesh, in_specs=placed, out_specs=P(("wide", "head"), None), check_vma=False
    )
```

```python
import functools
import math

import jax
import jax.numpy as jnp
from jax import lax
from jax.experimental import pallas as pl
from jax.experimental.pallas import tpu as pltpu
from jax.sharding import PartitionSpec as P

HD = 128
BLK = 128
PACKED = 16
GROUP = 4
DEAD = -1e30
MIB = 1024 * 1024
WHILE_EXCHANGING = pl.CostEstimate(flops=20 * 10**9, bytes_accessed=64 * MIB, transcendentals=0)

VMEM = pl.BlockSpec(memory_space=pltpu.VMEM)
HBM = pl.BlockSpec(memory_space=pltpu.HBM)


def in_hbm(arrays):
    return [pltpu.with_memory_space_constraint(a, pltpu.HBM) for a in arrays]


def like(array):
    return jax.ShapeDtypeStruct(array.shape, array.dtype)


def copies(pairs, sems):
    return [
        pltpu.make_async_copy(source, target, sems.at[i])
        for i, (source, target) in enumerate(pairs)
    ]


def pack_kernel(query_hbm, key_hbm, value_hbm, parent_hbm, packed_ref, parent_ref, sems):
    rows, width = query_hbm.shape
    kv_width = key_hbm.shape[1]
    moves = copies(
        (
            (parent_hbm, parent_ref),
            (query_hbm, packed_ref.at[:, pl.ds(0, width)]),
            (key_hbm, packed_ref.at[:, pl.ds(width, kv_width)]),
            (value_hbm, packed_ref.at[:, pl.ds(width + kv_width, kv_width)]),
        ),
        sems,
    )
    for move in moves:
        move.start()
    moves[0].wait()
    first = lax.axis_index("wide") * rows
    row = lax.broadcasted_iota(jnp.int32, (rows, HD), 0)
    parent = jnp.zeros((rows, HD), jnp.int32)
    for r in range(rows):
        parent = jnp.where(row == r, parent_ref[r] - first, parent)
    packed_ref[:, width + 2 * kv_width :] = parent.astype(jnp.float32).astype(jnp.bfloat16)
    for move in moves[1:]:
        move.wait()


def attend_kernel(groups, per_group, shift, packed_ref, pool_ref, owner_ref, *refs):
    out_ref = refs[-1]
    rows = packed_ref.shape[0]
    kv_width = groups * HD
    width = kv_width * per_group
    spots = owner_ref.shape[0]
    f32, bf16 = jnp.float32, jnp.bfloat16

    query = packed_ref[:, :width].astype(f32)
    tall = []
    for g in range(groups):
        heads = range(g * per_group, (g + 1) * per_group)
        block = jnp.concatenate([query[:, j * HD : (j + 1) * HD] for j in heads], axis=0)
        gap = jnp.zeros_like(block)
        tall.append(jnp.concatenate([block if i == g else gap for i in range(groups)], axis=1))
    tall = jnp.concatenate(tall, axis=0).astype(bf16)
    lanes = tall.shape[0]

    branch = lax.broadcasted_iota(jnp.int32, (1, lanes), 1) % rows
    code = packed_ref[:, width + 2 * kv_width :].astype(f32) + shift
    parent = jnp.zeros((1, lanes), f32)
    for r in range(rows):
        parent = jnp.where(branch == r, code[r : r + 1, :], parent)
    gap = jnp.zeros((PACKED - rows, kv_width), f32)
    key_own, value_own = (
        jnp.concatenate([packed_ref[:, start : start + kv_width].astype(f32), gap], axis=0).astype(bf16)
        for start in (width, width + kv_width)
    )
    of_branch = lax.broadcasted_iota(jnp.int32, (PACKED, lanes), 0) == branch

    def against(keys):
        return lax.dot_general(keys, tall, (((1,), (1,)), ((), ())), preferred_element_type=f32)

    def mixed(weights, values):
        return lax.dot_general(
            weights, values, (((0,), (0,)), ((), ())), preferred_element_type=f32
        )

    factor = 1.0 / math.sqrt(HD)
    scores = against(pool_ref[0].reshape(spots, kv_width)) * factor
    scores = jnp.where(owner_ref[...] == parent, scores, DEAD)
    own = jnp.sum(jnp.where(of_branch, against(key_own), 0.0), axis=0, keepdims=True) * factor
    top = jnp.maximum(jnp.max(scores, axis=0, keepdims=True), own)
    expo = jnp.exp(scores - top)
    own_expo = jnp.exp(own - top)
    share = 1.0 / (jnp.sum(expo, axis=0, keepdims=True) + own_expo)
    mixture = mixed((expo * share).astype(bf16), pool_ref[1].reshape(spots, kv_width))
    own_weight = jnp.where(of_branch, own_expo * share, 0.0).astype(bf16)
    mixture = mixture + mixed(own_weight, value_own)
    here = (code[:, :1] >= 0) & (code[:, :1] < rows)
    for j in range(groups * per_group):
        g = j // per_group
        out_ref[:, j * HD : (j + 1) * HD] = jnp.where(
            here, mixture[j * rows : (j + 1) * rows, g * HD : (g + 1) * HD], 0.0
        ).astype(bf16)


def side_by_side(block):
    height, width = block.shape
    per_row = HD // width
    wide = jnp.concatenate([block, jnp.zeros((height, HD - width), block.dtype)], axis=1)
    rows = []
    for start in range(0, height, per_row):
        row = wide[start : start + 1]
        for j in range(1, min(per_row, height - start)):
            row = row + pltpu.roll(wide[start + j : start + j + 1], j * width, 1)
        rows.append(row)
    return jnp.concatenate(rows, axis=0)


def prepare_kernel(count, *refs):
    page_hbm, length_hbm, sources = refs[0], refs[1], refs[2 : 2 + count]
    lists, refs = refs[2 + count : 7 + count], refs[7 + count :]
    owner_ref, targets, keeps_ref, scales_ref = refs[0], refs[1 : 1 + count], *refs[1 + count : 3 + count]
    page_ref, length_ref, keeps, scales, sems = refs[3 + count :]
    stacked = [keeps.at[i] for i in range(2)] + [scales.at[i] for i in range(3)]
    moves = copies(
        (
            (page_hbm, page_ref),
            (length_hbm, length_ref),
            *zip(sources, targets),
            *zip(lists, stacked),
        ),
        sems,
    )
    for move in moves:
        move.start()
    moves[0].wait()
    moves[1].wait()
    page = sources[0].shape[2]
    offset = lax.broadcasted_iota(jnp.int32, (page, HD), 0)
    for r in range(page_ref.shape[0]):
        for i in range(page_ref.shape[1]):
            places = pl.ds(pl.multiple_of(page_ref[r, i] * page, page), page)
            owner_ref[places, :] = jnp.where(offset < length_ref[r] - i * page, float(r), -1.0)
    for move in moves[2:]:
        move.wait()
    for source, target in ((keeps, keeps_ref), (scales, scales_ref)):
        for i in range(source.shape[0]):
            target[i] = side_by_side(source[i])


def merge_kernel(own_ref, behind_ref, residual_ref, cross_ref, stay_ref):
    head = lax.axis_index("head")
    part, width = cross_ref.shape
    both = own_ref[...].astype(jnp.float32) + behind_ref[...].astype(jnp.float32)
    low, high = both[:part], both[part : 2 * part]
    cross_ref[...] = jnp.where(head == 0, high, low).astype(jnp.bfloat16)
    stay_ref[:, :width] = jnp.where(head == 0, low, high).astype(jnp.bfloat16)
    stay_ref[:, width:] = residual_ref[...]


def norm_kernel(stay_ref, cross_ref, far_stay_ref, far_cross_ref, gain_ref, middle_ref, normed_ref):
    head = lax.axis_index("head")
    part, half = cross_ref.shape
    f32 = jnp.float32
    for i, (stay, cross) in enumerate(((stay_ref, cross_ref), (far_stay_ref, far_cross_ref))):
        same, other = stay[:, :half].astype(f32), cross[...].astype(f32)
        low = stay[:, half : 2 * half].astype(f32) + jnp.where(head == 0, same, other)
        high = stay[:, 2 * half :].astype(f32) + jnp.where(head == 0, other, same)
        if i == 0:
            middle_ref[:, :half] = low
            middle_ref[:, half:] = high
        square = jnp.sum(low * low, axis=-1, keepdims=True)
        square = square + jnp.sum(high * high, axis=-1, keepdims=True)
        scale = lax.rsqrt(square / (2 * half) + 1e-05)
        rows = slice(i * part, (i + 1) * part)
        normed_ref[rows, :half] = (low * scale * gain_ref[:, :half]).astype(jnp.bfloat16)
        normed_ref[rows, half:] = (high * scale * gain_ref[:, half:]).astype(jnp.bfloat16)


def feed_kernel(
    keeps_vmem, scales_vmem, near_ref, far_ref, gate_ref, up_ref, down_ref,
    stay_ref, send_ref, far_total, keeps_ref, scales_ref, sems,
):
    columns, keep = gate_ref.shape[:2]
    half = near_ref.shape[0]
    per_row = HD // keep
    moves = copies(((keeps_vmem, keeps_ref), (scales_vmem, scales_ref)), sems)
    for move in moves:
        move.start()
    stay_ref[...] = jnp.zeros_like(stay_ref)
    far_total[...] = jnp.zeros_like(far_total)
    for move in moves:
        move.wait()

    def entry(ref, which, c, k):
        return ref[which, c // per_row, c % per_row * keep + k]

    def block(which, c, k):
        return pl.ds(pl.multiple_of(entry(keeps_ref, which, c, k) * BLK, BLK), BLK)

    hidden = []
    for c in range(columns):
        gate_sum = jnp.zeros((2 * half, BLK), jnp.float32)
        up_sum = jnp.zeros((2 * half, BLK), jnp.float32)
        for k in range(keep):
            where = block(0, c, k)
            picked = jnp.concatenate([near_ref[:, where], far_ref[:, where]], axis=0)
            both = jnp.dot(
                picked, jnp.concatenate([gate_ref[c, k], up_ref[c, k]], axis=1),
                preferred_element_type=jnp.float32,
            )
            gate_sum += entry(scales_ref, 0, c, k) * both[:, :BLK]
            up_sum += entry(scales_ref, 1, c, k) * both[:, BLK:]
        hidden.append((gate_sum / (1.0 + jnp.exp(-gate_sum)) * up_sum).astype(jnp.bfloat16))
    for c in range(columns):
        for start in range(0, keep, GROUP):
            group = range(start, start + GROUP)
            places = [block(1, c, k) for k in group]
            near_sums = [stay_ref[:, where] for where in places]
            far_sums = [far_total[:, where] for where in places]
            for i in range(0, GROUP, 2):
                both = jnp.dot(
                    hidden[c],
                    jnp.concatenate([down_ref[c, group[i]], down_ref[c, group[i + 1]]], axis=1),
                    preferred_element_type=jnp.float32,
                )
                for j in range(2):
                    term = entry(scales_ref, 2, c, group[i + j]) * both[:, j * BLK : (j + 1) * BLK]
                    near_sums[i + j] += term[:half]
                    far_sums[i + j] += term[half:]
            for where, near_sum, far_sum in zip(places, near_sums, far_sums):
                stay_ref[:, where] = near_sum
                far_total[:, where] = far_sum
    send_ref[...] = far_total[...].astype(jnp.bfloat16)


def join_kernel(*refs):
    out_ref = refs[-1]
    height = refs[0].shape[0]
    for i, ref in enumerate(refs[:-1]):
        out_ref[i * height : (i + 1) * height, :] = ref[...]


def joined(blocks):
    height, width = blocks[0].shape
    return pl.pallas_call(
        join_kernel,
        out_shape=jax.ShapeDtypeStruct((len(blocks) * height, width), blocks[0].dtype),
        in_specs=[VMEM] * len(blocks),
        out_specs=VMEM,
        compiler_params=pltpu.CompilerParams(vmem_limit_bytes=2 * MIB),
        name="join",
    )(*blocks)


def sum_kernel(count, kept_ref, *refs):
    blocks, kept_out, sent = refs[:count], refs[count], refs[count + 1 :]
    height = kept_out.shape[0]
    for i, out_ref in enumerate((kept_out, *sent)):
        rows = slice(i * height, (i + 1) * height)
        total = kept_ref[rows, :]
        for block in blocks:
            total = total + block[rows, :].astype(jnp.float32)
        out_ref[...] = total.astype(out_ref.dtype)


def summed(kept, blocks, parts):
    height, width = kept.shape
    part = (height // parts, width)
    return pl.pallas_call(
        functools.partial(sum_kernel, len(blocks)),
        out_shape=(
            jax.ShapeDtypeStruct(part, jnp.float32),
            *[jax.ShapeDtypeStruct(part, jnp.bfloat16)] * (parts - 1),
        ),
        in_specs=[VMEM] * (1 + len(blocks)),
        out_specs=(VMEM,) * parts,
        compiler_params=pltpu.CompilerParams(vmem_limit_bytes=2 * MIB),
        name="sum",
    )(kept, *blocks)


def swapped(block, bits):
    return lax.ppermute(block, "wide", [(i, i ^ bits) for i in range(lax.axis_size("wide"))])


def combined(bits):
    sums = [0]
    for bit in bits:
        sums += [s + bit for s in sums]
    return sums[1:]


def per_device(
    branch_query, key_new, value_new, pool_pages, page_table, tail_length, parent_row, residual,
    norm_gain, gate_blocks, up_blocks, gate_up_keep, gate_scale, up_scale, down_blocks, down_keep,
    down_scale,
):
    bf16, f32 = jnp.bfloat16, jnp.float32
    wide, heads = lax.axis_size("wide"), lax.axis_size("head")
    rows, width = branch_query.shape
    kv_width = key_new.shape[1]
    groups = kv_width // HD
    per_group = width // kv_width
    part, model = residual.shape
    columns, keep = gate_up_keep.shape

    own = pl.pallas_call(
        pack_kernel,
        out_shape=jax.ShapeDtypeStruct((rows, width + 2 * kv_width + HD), bf16),
        in_specs=[HBM] * 4,
        out_specs=VMEM,
        scratch_shapes=[
            pltpu.SMEM(parent_row.shape, jnp.int32),
            pltpu.SemaphoreType.DMA((4,)),
        ],
        compiler_params=pltpu.CompilerParams(vmem_limit_bytes=2 * MIB),
        name="pack",
    )(*in_hbm([branch_query, key_new, value_new, parent_row]))
    following = lax.ppermute(own, "wide", [(i, i - 1) for i in range(1, wide)])

    stored = [pool_pages, residual, norm_gain.reshape(1, model)]
    lists = [gate_up_keep, down_keep, gate_scale, up_scale, down_scale]
    spots = pool_pages.shape[1] * pool_pages.shape[2]
    owner, pool, residual, gain, keeps, scales = pl.pallas_call(
        functools.partial(prepare_kernel, len(stored)),
        out_shape=(
            jax.ShapeDtypeStruct((spots, HD), f32),
            *[like(a) for a in stored],
            jax.ShapeDtypeStruct((2, -(-columns * keep // HD), HD), jnp.int32),
            jax.ShapeDtypeStruct((3, -(-columns * keep // HD), HD), f32),
        ),
        in_specs=[HBM] * (2 + len(stored) + len(lists)),
        out_specs=(VMEM,) * (3 + len(stored)),
        scratch_shapes=[
            pltpu.SMEM(page_table.shape, jnp.int32),
            pltpu.SMEM(tail_length.shape, jnp.int32),
            pltpu.VMEM((2, columns, keep), jnp.int32),
            pltpu.VMEM((3, columns, keep), f32),
            pltpu.SemaphoreType.DMA((2 + len(stored) + len(lists),)),
        ],
        compiler_params=pltpu.CompilerParams(vmem_limit_bytes=2 * MIB),
        cost_estimate=pl.CostEstimate(flops=0, bytes_accessed=8 * MIB, transcendentals=0),
        name="prepare",
    )(*in_hbm([page_table, tail_length, *stored, *lists]))

    def attended(packed, shift, *after):
        return pl.pallas_call(
            functools.partial(attend_kernel, groups, per_group, shift),
            out_shape=jax.ShapeDtypeStruct((rows, width), bf16),
            in_specs=[VMEM] * (3 + len(after)),
            out_specs=VMEM,
            compiler_params=pltpu.CompilerParams(vmem_limit_bytes=6 * MIB),
            name="attend",
        )(packed, pool, owner, *after)

    ahead = attended(following, rows)
    behind = lax.ppermute(ahead, "wide", [(i, i + 1) for i in range(wide - 1)])
    mixed = attended(own, 0, ahead)
    bits = [1 << b for b in range(wide.bit_length() - 1)]
    stages = [(bits[0],), tuple(bits[1:3]), *[(bit,) for bit in bits[3:]]]
    sum_stages = stages[1:]
    high = bits[-1]
    cross, stay = pl.pallas_call(
        merge_kernel,
        out_shape=(
            jax.ShapeDtypeStruct((part, width), bf16),
            jax.ShapeDtypeStruct((part, width + model), bf16),
        ),
        in_specs=[VMEM] * 3,
        out_specs=(VMEM,) * 2,
        compiler_params=pltpu.CompilerParams(vmem_limit_bytes=2 * MIB),
        cost_estimate=WHILE_EXCHANGING,
        name="merge",
    )(mixed, behind, residual)
    far_cross = lax.ppermute(
        cross,
        ("wide", "head"),
        [(i * heads + h, (i ^ high) * heads + 1 - h) for i in range(wide) for h in range(heads)],
    )
    far_stay = swapped(stay, high)
    near_cross = lax.ppermute(cross, "head", [(h, 1 - h) for h in range(heads)])
    middle, gathered = pl.pallas_call(
        norm_kernel,
        out_shape=(
            jax.ShapeDtypeStruct((part, model), f32),
            jax.ShapeDtypeStruct((2 * part, model), bf16),
        ),
        in_specs=[VMEM] * 5,
        out_specs=(VMEM,) * 2,
        compiler_params=pltpu.CompilerParams(vmem_limit_bytes=2 * MIB),
        name="norm",
    )(stay, near_cross, far_stay, far_cross, gain)
    for stage in stages[-2:0:-1]:
        gathered = joined([gathered] + [swapped(gathered, s) for s in combined(stage)])
    far = swapped(gathered, bits[0])

    half = gathered.shape[0]
    kept, sent = pl.pallas_call(
        feed_kernel,
        out_shape=(
            jax.ShapeDtypeStruct((half, model), f32),
            jax.ShapeDtypeStruct((half, model), bf16),
        ),
        in_specs=[VMEM] * 7,
        out_specs=(VMEM,) * 2,
        scratch_shapes=[
            pltpu.VMEM((half, model), f32),
            pltpu.SMEM(keeps.shape, jnp.int32),
            pltpu.SMEM(scales.shape, f32),
            pltpu.SemaphoreType.DMA((2,)),
        ],
        compiler_params=pltpu.CompilerParams(vmem_limit_bytes=half * model * 10 + 6 * MIB),
        name="feed",
    )(keeps, scales, gathered, far, gate_blocks, up_blocks, down_blocks)

    blocks = [swapped(sent, bits[0])]
    for stage in sum_stages:
        sums = combined(stage)
        kept, *sent = summed(kept, blocks, 1 + len(sums))
        farthest = sorted(zip(sent, sums), key=lambda pair: -bin(pair[1]).count("1"))
        blocks = [swapped(block, s) for block, s in farthest]
    total = middle + kept
    for block in blocks:
        total = total + block.astype(f32)
    return total.astype(bf16)


def solution(mesh):
    placed = (
        P("wide", "head"),
        P("wide", "head"),
        P("wide", "head"),
        P(None, "wide", None, "head"),
        P("wide", None),
        P("wide"),
        P("wide"),
        P(("wide", "head"), None),
        P(),
        P("wide", None, None, None),
        P("wide", None, None, None),
        P("wide", None),
        P("wide", None),
        P("wide", None),
        P("wide", None, None, None),
        P("wide", None),
        P("wide", None),
    )
    return jax.shard_map(
        per_device, mesh=mesh, in_specs=placed, out_specs=P(("wide", "head"), None), check_vma=False
    )
```

```python
import functools
import math

import jax
import jax.numpy as jnp
from jax import lax
from jax.experimental import pallas as pl
from jax.experimental.pallas import tpu as pltpu
from jax.sharding import PartitionSpec as P

HD = 128
BLK = 128
PACKED = 16
GROUP = 2
DEAD = -1e30
MIB = 1024 * 1024
WHILE_EXCHANGING = pl.CostEstimate(flops=20 * 10**9, bytes_accessed=64 * MIB, transcendentals=0)

VMEM = pl.BlockSpec(memory_space=pltpu.VMEM)
HBM = pl.BlockSpec(memory_space=pltpu.HBM)


def in_hbm(arrays):
    return [pltpu.with_memory_space_constraint(a, pltpu.HBM) for a in arrays]


def like(array):
    return jax.ShapeDtypeStruct(array.shape, array.dtype)


def copies(pairs, sems):
    return [
        pltpu.make_async_copy(source, target, sems.at[i])
        for i, (source, target) in enumerate(pairs)
    ]


def pack_kernel(query_hbm, key_hbm, value_hbm, parent_hbm, packed_ref, parent_ref, sems):
    rows, width = query_hbm.shape
    kv_width = key_hbm.shape[1]
    moves = copies(
        (
            (parent_hbm, parent_ref),
            (query_hbm, packed_ref.at[:, pl.ds(0, width)]),
            (key_hbm, packed_ref.at[:, pl.ds(width, kv_width)]),
            (value_hbm, packed_ref.at[:, pl.ds(width + kv_width, kv_width)]),
        ),
        sems,
    )
    for move in moves:
        move.start()
    moves[0].wait()
    first = lax.axis_index("wide") * rows
    row = lax.broadcasted_iota(jnp.int32, (rows, HD), 0)
    parent = jnp.zeros((rows, HD), jnp.int32)
    for r in range(rows):
        parent = jnp.where(row == r, parent_ref[r] - first, parent)
    packed_ref[:, width + 2 * kv_width :] = parent.astype(jnp.float32).astype(jnp.bfloat16)
    for move in moves[1:]:
        move.wait()


def attend_kernel(groups, per_group, shift, packed_ref, pool_ref, owner_ref, *refs):
    out_ref = refs[-1]
    rows = packed_ref.shape[0]
    kv_width = groups * HD
    width = kv_width * per_group
    spots = owner_ref.shape[0]
    f32, bf16 = jnp.float32, jnp.bfloat16

    query = packed_ref[:, :width].astype(f32)
    tall = []
    for g in range(groups):
        heads = range(g * per_group, (g + 1) * per_group)
        block = jnp.concatenate([query[:, j * HD : (j + 1) * HD] for j in heads], axis=0)
        gap = jnp.zeros_like(block)
        tall.append(jnp.concatenate([block if i == g else gap for i in range(groups)], axis=1))
    tall = jnp.concatenate(tall, axis=0).astype(bf16)
    lanes = tall.shape[0]

    branch = lax.broadcasted_iota(jnp.int32, (1, lanes), 1) % rows
    code = packed_ref[:, width + 2 * kv_width :].astype(f32) + shift
    parent = jnp.zeros((1, lanes), f32)
    for r in range(rows):
        parent = jnp.where(branch == r, code[r : r + 1, :], parent)
    gap = jnp.zeros((PACKED - rows, kv_width), f32)
    key_own, value_own = (
        jnp.concatenate([packed_ref[:, start : start + kv_width].astype(f32), gap], axis=0).astype(bf16)
        for start in (width, width + kv_width)
    )
    of_branch = lax.broadcasted_iota(jnp.int32, (PACKED, lanes), 0) == branch

    def against(keys):
        return lax.dot_general(keys, tall, (((1,), (1,)), ((), ())), preferred_element_type=f32)

    def mixed(weights, values):
        return lax.dot_general(
            weights, values, (((0,), (0,)), ((), ())), preferred_element_type=f32
        )

    factor = 1.0 / math.sqrt(HD)
    scores = against(pool_ref[0].reshape(spots, kv_width)) * factor
    scores = jnp.where(owner_ref[...] == parent, scores, DEAD)
    own = jnp.sum(jnp.where(of_branch, against(key_own), 0.0), axis=0, keepdims=True) * factor
    top = jnp.maximum(jnp.max(scores, axis=0, keepdims=True), own)
    expo = jnp.exp(scores - top)
    own_expo = jnp.exp(own - top)
    share = 1.0 / (jnp.sum(expo, axis=0, keepdims=True) + own_expo)
    mixture = mixed((expo * share).astype(bf16), pool_ref[1].reshape(spots, kv_width))
    own_weight = jnp.where(of_branch, own_expo * share, 0.0).astype(bf16)
    mixture = mixture + mixed(own_weight, value_own)
    here = (code[:, :1] >= 0) & (code[:, :1] < rows)
    for j in range(groups * per_group):
        g = j // per_group
        out_ref[:, j * HD : (j + 1) * HD] = jnp.where(
            here, mixture[j * rows : (j + 1) * rows, g * HD : (g + 1) * HD], 0.0
        ).astype(bf16)


def side_by_side(block):
    height, width = block.shape
    per_row = HD // width
    wide = jnp.concatenate([block, jnp.zeros((height, HD - width), block.dtype)], axis=1)
    rows = []
    for start in range(0, height, per_row):
        row = wide[start : start + 1]
        for j in range(1, min(per_row, height - start)):
            row = row + pltpu.roll(wide[start + j : start + j + 1], j * width, 1)
        rows.append(row)
    return jnp.concatenate(rows, axis=0)


def prepare_kernel(count, *refs):
    page_hbm, length_hbm, sources = refs[0], refs[1], refs[2 : 2 + count]
    lists, refs = refs[2 + count : 7 + count], refs[7 + count :]
    owner_ref, targets, keeps_ref, scales_ref = refs[0], refs[1 : 1 + count], *refs[1 + count : 3 + count]
    page_ref, length_ref, keeps, scales, sems = refs[3 + count :]
    stacked = [keeps.at[i] for i in range(2)] + [scales.at[i] for i in range(3)]
    moves = copies(
        (
            (page_hbm, page_ref),
            (length_hbm, length_ref),
            *zip(sources, targets),
            *zip(lists, stacked),
        ),
        sems,
    )
    for move in moves:
        move.start()
    moves[0].wait()
    moves[1].wait()
    page = sources[0].shape[2]
    offset = lax.broadcasted_iota(jnp.int32, (page, HD), 0)
    for r in range(page_ref.shape[0]):
        for i in range(page_ref.shape[1]):
            places = pl.ds(pl.multiple_of(page_ref[r, i] * page, page), page)
            owner_ref[places, :] = jnp.where(offset < length_ref[r] - i * page, float(r), -1.0)
    for move in moves[2:]:
        move.wait()
    for source, target in ((keeps, keeps_ref), (scales, scales_ref)):
        for i in range(source.shape[0]):
            target[i] = side_by_side(source[i])


def merge_kernel(own_ref, behind_ref, residual_ref, cross_ref, stay_ref):
    head = lax.axis_index("head")
    part, width = cross_ref.shape
    both = own_ref[...].astype(jnp.float32) + behind_ref[...].astype(jnp.float32)
    low, high = both[:part], both[part : 2 * part]
    cross_ref[...] = jnp.where(head == 0, high, low).astype(jnp.bfloat16)
    stay_ref[:, :width] = jnp.where(head == 0, low, high).astype(jnp.bfloat16)
    stay_ref[:, width:] = residual_ref[...]


def norm_kernel(stay_ref, cross_ref, far_stay_ref, far_cross_ref, gain_ref, middle_ref, normed_ref):
    head = lax.axis_index("head")
    part, half = cross_ref.shape
    f32 = jnp.float32
    for i, (stay, cross) in enumerate(((stay_ref, cross_ref), (far_stay_ref, far_cross_ref))):
        same, other = stay[:, :half].astype(f32), cross[...].astype(f32)
        low = stay[:, half : 2 * half].astype(f32) + jnp.where(head == 0, same, other)
        high = stay[:, 2 * half :].astype(f32) + jnp.where(head == 0, other, same)
        if i == 0:
            middle_ref[:, :half] = low
            middle_ref[:, half:] = high
        square = jnp.sum(low * low, axis=-1, keepdims=True)
        square = square + jnp.sum(high * high, axis=-1, keepdims=True)
        scale = lax.rsqrt(square / (2 * half) + 1e-05)
        rows = slice(i * part, (i + 1) * part)
        normed_ref[rows, :half] = (low * scale * gain_ref[:, :half]).astype(jnp.bfloat16)
        normed_ref[rows, half:] = (high * scale * gain_ref[:, half:]).astype(jnp.bfloat16)


def feed_kernel(
    keeps_vmem, scales_vmem, near_ref, far_ref, gate_ref, up_ref, down_ref,
    stay_ref, send_ref, far_total, keeps_ref, scales_ref, sems,
):
    columns, keep = gate_ref.shape[:2]
    half = near_ref.shape[0]
    per_row = HD // keep
    moves = copies(((keeps_vmem, keeps_ref), (scales_vmem, scales_ref)), sems)
    for move in moves:
        move.start()
    moves[0].wait()
    stay_ref[...] = jnp.zeros_like(stay_ref)
    far_total[...] = jnp.zeros_like(far_total)
    moves[1].wait()

    def entry(ref, which, c, k):
        return ref[which, c // per_row, c % per_row * keep + k]

    def block(which, c, k):
        return pl.ds(pl.multiple_of(entry(keeps_ref, which, c, k) * BLK, BLK), BLK)

    hidden = []
    for c in range(columns):
        gate_sum = jnp.zeros((2 * half, BLK), jnp.float32)
        up_sum = jnp.zeros((2 * half, BLK), jnp.float32)
        for k in range(keep):
            where = block(0, c, k)
            picked = jnp.concatenate([near_ref[:, where], far_ref[:, where]], axis=0)
            both = jnp.dot(
                picked, jnp.concatenate([gate_ref[c, k], up_ref[c, k]], axis=1),
                preferred_element_type=jnp.float32,
            )
            gate_sum += entry(scales_ref, 0, c, k) * both[:, :BLK]
            up_sum += entry(scales_ref, 1, c, k) * both[:, BLK:]
        hidden.append((gate_sum / (1.0 + jnp.exp(-gate_sum)) * up_sum).astype(jnp.bfloat16))
    for c in range(columns):
        for start in range(0, keep, GROUP):
            group = range(start, start + GROUP)
            places = [block(1, c, k) for k in group]
            near_sums = [stay_ref[:, where] for where in places]
            far_sums = [far_total[:, where] for where in places]
            for i in range(0, GROUP, 2):
                both = jnp.dot(
                    hidden[c],
                    jnp.concatenate([down_ref[c, group[i]], down_ref[c, group[i + 1]]], axis=1),
                    preferred_element_type=jnp.float32,
                )
                for j in range(2):
                    term = entry(scales_ref, 2, c, group[i + j]) * both[:, j * BLK : (j + 1) * BLK]
                    near_sums[i + j] += term[:half]
                    far_sums[i + j] += term[half:]
            for where, near_sum, far_sum in zip(places, near_sums, far_sums):
                stay_ref[:, where] = near_sum
                far_total[:, where] = far_sum
    send_ref[...] = far_total[...].astype(jnp.bfloat16)


def join_kernel(*refs):
    out_ref = refs[-1]
    height = refs[0].shape[0]
    for i, ref in enumerate(refs[:-1]):
        out_ref[i * height : (i + 1) * height, :] = ref[...]


def joined(blocks):
    height, width = blocks[0].shape
    return pl.pallas_call(
        join_kernel,
        out_shape=jax.ShapeDtypeStruct((len(blocks) * height, width), blocks[0].dtype),
        in_specs=[VMEM] * len(blocks),
        out_specs=VMEM,
        compiler_params=pltpu.CompilerParams(vmem_limit_bytes=2 * MIB),
        name="join",
    )(*blocks)


def sum_kernel(count, kept_ref, *refs):
    blocks, kept_out, sent = refs[:count], refs[count], refs[count + 1 :]
    height = kept_out.shape[0]
    for i, out_ref in enumerate((kept_out, *sent)):
        rows = slice(i * height, (i + 1) * height)
        total = kept_ref[rows, :]
        for block in blocks:
            total = total + block[rows, :].astype(jnp.float32)
        out_ref[...] = total.astype(out_ref.dtype)


def summed(kept, blocks, parts):
    height, width = kept.shape
    part = (height // parts, width)
    return pl.pallas_call(
        functools.partial(sum_kernel, len(blocks)),
        out_shape=(
            jax.ShapeDtypeStruct(part, jnp.float32),
            *[jax.ShapeDtypeStruct(part, jnp.bfloat16)] * (parts - 1),
        ),
        in_specs=[VMEM] * (1 + len(blocks)),
        out_specs=(VMEM,) * parts,
        compiler_params=pltpu.CompilerParams(vmem_limit_bytes=2 * MIB),
        name="sum",
    )(kept, *blocks)


def swapped(block, bits):
    return lax.ppermute(block, "wide", [(i, i ^ bits) for i in range(lax.axis_size("wide"))])


def combined(bits):
    sums = [0]
    for bit in bits:
        sums += [s + bit for s in sums]
    return sums[1:]


def per_device(
    branch_query, key_new, value_new, pool_pages, page_table, tail_length, parent_row, residual,
    norm_gain, gate_blocks, up_blocks, gate_up_keep, gate_scale, up_scale, down_blocks, down_keep,
    down_scale,
):
    bf16, f32 = jnp.bfloat16, jnp.float32
    wide, heads = lax.axis_size("wide"), lax.axis_size("head")
    rows, width = branch_query.shape
    kv_width = key_new.shape[1]
    groups = kv_width // HD
    per_group = width // kv_width
    part, model = residual.shape
    columns, keep = gate_up_keep.shape

    own = pl.pallas_call(
        pack_kernel,
        out_shape=jax.ShapeDtypeStruct((rows, width + 2 * kv_width + HD), bf16),
        in_specs=[HBM] * 4,
        out_specs=VMEM,
        scratch_shapes=[
            pltpu.SMEM(parent_row.shape, jnp.int32),
            pltpu.SemaphoreType.DMA((4,)),
        ],
        compiler_params=pltpu.CompilerParams(vmem_limit_bytes=2 * MIB),
        name="pack",
    )(*in_hbm([branch_query, key_new, value_new, parent_row]))
    following = lax.ppermute(own, "wide", [(i, i - 1) for i in range(1, wide)])

    stored = [pool_pages, residual, norm_gain.reshape(1, model)]
    lists = [gate_up_keep, down_keep, gate_scale, up_scale, down_scale]
    spots = pool_pages.shape[1] * pool_pages.shape[2]
    owner, pool, residual, gain, keeps, scales = pl.pallas_call(
        functools.partial(prepare_kernel, len(stored)),
        out_shape=(
            jax.ShapeDtypeStruct((spots, HD), f32),
            *[like(a) for a in stored],
            jax.ShapeDtypeStruct((2, -(-columns * keep // HD), HD), jnp.int32),
            jax.ShapeDtypeStruct((3, -(-columns * keep // HD), HD), f32),
        ),
        in_specs=[HBM] * (2 + len(stored) + len(lists)),
        out_specs=(VMEM,) * (3 + len(stored)),
        scratch_shapes=[
            pltpu.SMEM(page_table.shape, jnp.int32),
            pltpu.SMEM(tail_length.shape, jnp.int32),
            pltpu.VMEM((2, columns, keep), jnp.int32),
            pltpu.VMEM((3, columns, keep), f32),
            pltpu.SemaphoreType.DMA((2 + len(stored) + len(lists),)),
        ],
        compiler_params=pltpu.CompilerParams(vmem_limit_bytes=2 * MIB),
        cost_estimate=pl.CostEstimate(flops=0, bytes_accessed=8 * MIB, transcendentals=0),
        name="prepare",
    )(*in_hbm([page_table, tail_length, *stored, *lists]))

    def attended(packed, shift, *after):
        return pl.pallas_call(
            functools.partial(attend_kernel, groups, per_group, shift),
            out_shape=jax.ShapeDtypeStruct((rows, width), bf16),
            in_specs=[VMEM] * (3 + len(after)),
            out_specs=VMEM,
            compiler_params=pltpu.CompilerParams(vmem_limit_bytes=6 * MIB),
            name="attend",
        )(packed, pool, owner, *after)

    ahead = attended(following, rows)
    behind = lax.ppermute(ahead, "wide", [(i, i + 1) for i in range(wide - 1)])
    mixed = attended(own, 0, ahead)
    bits = [1 << b for b in range(wide.bit_length() - 1)]
    stages = [(bits[0],), tuple(bits[1:3]), *[(bit,) for bit in bits[3:]]]
    sum_stages = stages[1:]
    high = bits[-1]
    cross, stay = pl.pallas_call(
        merge_kernel,
        out_shape=(
            jax.ShapeDtypeStruct((part, width), bf16),
            jax.ShapeDtypeStruct((part, width + model), bf16),
        ),
        in_specs=[VMEM] * 3,
        out_specs=(VMEM,) * 2,
        compiler_params=pltpu.CompilerParams(vmem_limit_bytes=2 * MIB),
        cost_estimate=WHILE_EXCHANGING,
        name="merge",
    )(mixed, behind, residual)
    far_cross = lax.ppermute(
        cross,
        ("wide", "head"),
        [(i * heads + h, (i ^ high) * heads + 1 - h) for i in range(wide) for h in range(heads)],
    )
    far_stay = swapped(stay, high)
    near_cross = lax.ppermute(cross, "head", [(h, 1 - h) for h in range(heads)])
    middle, gathered = pl.pallas_call(
        norm_kernel,
        out_shape=(
            jax.ShapeDtypeStruct((part, model), f32),
            jax.ShapeDtypeStruct((2 * part, model), bf16),
        ),
        in_specs=[VMEM] * 5,
        out_specs=(VMEM,) * 2,
        compiler_params=pltpu.CompilerParams(vmem_limit_bytes=2 * MIB),
        name="norm",
    )(stay, near_cross, far_stay, far_cross, gain)
    for stage in stages[-2:0:-1]:
        gathered = joined([gathered] + [swapped(gathered, s) for s in combined(stage)])
    far = swapped(gathered, bits[0])

    half = gathered.shape[0]
    kept, sent = pl.pallas_call(
        feed_kernel,
        out_shape=(
            jax.ShapeDtypeStruct((half, model), f32),
            jax.ShapeDtypeStruct((half, model), bf16),
        ),
        in_specs=[VMEM] * 7,
        out_specs=(VMEM,) * 2,
        scratch_shapes=[
            pltpu.VMEM((half, model), f32),
            pltpu.SMEM(keeps.shape, jnp.int32),
            pltpu.SMEM(scales.shape, f32),
            pltpu.SemaphoreType.DMA((2,)),
        ],
        compiler_params=pltpu.CompilerParams(vmem_limit_bytes=half * model * 10 + 6 * MIB),
        name="feed",
    )(keeps, scales, gathered, far, gate_blocks, up_blocks, down_blocks)

    blocks = [swapped(sent, bits[0])]
    for stage in sum_stages:
        sums = combined(stage)
        kept, *sent = summed(kept, blocks, 1 + len(sums))
        farthest = sorted(zip(sent, sums), key=lambda pair: -bin(pair[1]).count("1"))
        blocks = [swapped(block, s) for block, s in farthest]
    total = middle + kept
    for block in blocks:
        total = total + block.astype(f32)
    return total.astype(bf16)


def solution(mesh):
    placed = (
        P("wide", "head"),
        P("wide", "head"),
        P("wide", "head"),
        P(None, "wide", None, "head"),
        P("wide", None),
        P("wide"),
        P("wide"),
        P(("wide", "head"), None),
        P(),
        P("wide", None, None, None),
        P("wide", None, None, None),
        P("wide", None),
        P("wide", None),
        P("wide", None),
        P("wide", None, None, None),
        P("wide", None),
        P("wide", None),
    )
    return jax.shard_map(
        per_device, mesh=mesh, in_specs=placed, out_specs=P(("wide", "head"), None), check_vma=False
    )
```
